128 devices in a mesh: dp: 32 (over x, z_lo, y), tensor: 4 (over z_hi, core).
Axes of the slice: x: 4, y: 4, z: 4 (z_hi: 2, z_lo: 2; z = z_hi * 2 + z_lo), core: 2. Of those that a mesh axis runs over, the one named last changes fastest.
Arguments:
- tokens_in: bfloat16 [32, 512, 1024], P('dp'), may hold values from -6 to 6
- cotangent: bfloat16 [32, 512, 1024], P('dp'), may hold values from -6 to 6
- segment_ids: int32 [32, 512], P('dp'), may hold values from 0 to 3, never falling along the last dimension, each value on 1 to 256 neighbouring positions
- in_weight: float32 [3, 1024, 1024], P(None, 'dp', 'tensor'), may hold values from -0.1875 to 0.1875
- out_weight: float32 [1024, 1024], P('tensor', 'dp'), may hold values from -0.1875 to 0.1875
- gate_up_weight: float32 [2, 1024, 4608], P(None, 'dp', 'tensor'), may hold values from -0.1875 to 0.1875
- down_weight: float32 [4608, 1024], P('tensor', 'dp'), may hold values from -0.09375 to 0.09375
- conv_weight: float32 [3, 1024], P(None, 'tensor'), may hold values from -3 to 3
- norm_gains: float32 [2, 1024], P(None, 'dp'), may hold values from 0.5 to 1.5
- in_first: float32 [3, 1024, 1024], P(None, 'dp', 'tensor'), may hold values from -84.48 to 84.48
- in_second: float32 [3, 1024, 1024], P(None, 'dp', 'tensor'), may hold values from 861.7984 to 3440.64
- out_first: float32 [1024, 1024], P('tensor', 'dp'), may hold values from -107.52 to 107.52
- out_second: float32 [1024, 1024], P('tensor', 'dp'), may hold values from 1458.176 to 5832.704
- gate_up_first: float32 [2, 1024, 4608], P(None, 'dp', 'tensor'), may hold values from -25.6 to 25.6
- gate_up_second: float32 [2, 1024, 4608], P(None, 'dp', 'tensor'), may hold values from 77.0048 to 311.296
- down_first: float32 [4608, 1024], P('tensor', 'dp'), may hold values from -42.24 to 42.24
- down_second: float32 [4608, 1024], P('tensor', 'dp'), may hold values from 212.992 to 851.968
- conv_first: float32 [3, 1024], P(None, 'tensor'), may hold values from -107.52 to 107.52
- conv_second: float32 [3, 1024], P(None, 'tensor'), may hold values from 1458.176 to 5832.704
- gains_first: float32 [2, 1024], P(None, 'dp'), may hold values from -84.48 to 84.48
- gains_second: float32 [2, 1024], P(None, 'dp'), may hold values from 861.7984 to 3440.64
Outputs:
- block_out: float32 [32, 512, 1024], P('dp')
- tokens_grad: float32 [32, 512, 1024], P('dp')
- in_weight_new: float32 [3, 1024, 1024], P(None, 'dp', 'tensor')
- in_first_new: float32 [3, 1024, 1024], P(None, 'dp', 'tensor')
- in_second_new: float32 [3, 1024, 1024], P(None, 'dp', 'tensor')
- out_weight_new: float32 [1024, 1024], P('tensor', 'dp')
- out_first_new: float32 [1024, 1024], P('tensor', 'dp')
- out_second_new: float32 [1024, 1024], P('tensor', 'dp')
- gate_up_weight_new: float32 [2, 1024, 4608], P(None, 'dp', 'tensor')
- gate_up_first_new: float32 [2, 1024, 4608], P(None, 'dp', 'tensor')
- gate_up_second_new: float32 [2, 1024, 4608], P(None, 'dp', 'tensor')
- down_weight_new: float32 [4608, 1024], P('tensor', 'dp')
- down_first_new: float32 [4608, 1024], P('tensor', 'dp')
- down_second_new: float32 [4608, 1024], P('tensor', 'dp')
- conv_weight_new: float32 [3, 1024], P(None, 'tensor')
- conv_first_new: float32 [3, 1024], P(None, 'tensor')
- conv_second_new: float32 [3, 1024], P(None, 'tensor')
- norm_gains_new: float32 [2, 1024], P(None, 'dp')
- gains_first_new: float32 [2, 1024], P(None, 'dp')
- gains_second_new: float32 [2, 1024], P(None, 'dp')
The draws below stay inside these ranges and needn't reach their ends.
Inputs may be any that keep to these rules, and one draw needn't show every extreme that they name: `segment_ids`: segment ids never fall along a sequence; each document has 1 to 256 tokens and one has exactly 256.
All inputs are finite; a program needn't handle non-finite values.
Results may differ from the reference program's by a relative error of at most 0.012.
The reference program's roundings to bfloat16 on the way count: a program that leaves them out, or rounds other values in their place, can miss the bound.
Values may be sent and summed in bfloat16 or wider, within the bound.
No kernel may reach another device: no remote copies, remote signals or barrier semaphores. Data moves between devices by JAX's collectives and lax.ppermute only.
A program may use at most 128 MiB of HBM per device.

```python
import math
import jax
import jax.numpy as jnp
import numpy as np
from jax import lax

D = 1024
FF = 4608
TAPS = 3
ADAM_STEP = 10
SEQ = 512
SEQS = 32
DOCS = 4
DOC_MOST = 256
N_DP = 32


def steps_of(stream_key, extent, split, smallest, top_value):
    gain = 1.0
    for position, parts in split:
        heights = jax.random.uniform(jax.random.fold_in(jax.random.fold_in(stream_key, 6), position), (parts,), jnp.float32, smallest / len(split), top_value / len(split))
        gain = gain * jnp.repeat(jnp.exp(heights), extent[position] // parts).reshape((-1,) + (1,) * (len(extent) - 1 - position))
    return gain


def length_profile(number_of, total, reach, lean):
    portions = [(1 << 20) // math.isqrt(grade ** lean) + 1 for grade in range(2, number_of + 1)]
    spare, counts = total - reach - (number_of - 1), [1] * (number_of - 1)
    while spare > 0:
        free = [i for i in range(number_of - 1) if counts[i] < reach]
        whole, budget = sum([portions[i] for i in free]), spare
        for i in free:
            addition = min(reach - counts[i], max(1, budget * portions[i] // whole), spare)
            counts[i] = counts[i] + addition
            spare = spare - addition
    return np.array([reach] + counts)


def ragged_sizes(own_key, number_of, total, reach, slope):
    if number_of == 2:
        one = jax.random.randint(own_key, (), max(1, total - reach), min(reach, total - 1) + 1)
        return jnp.stack([one, total - one])
    lengths = jnp.asarray(length_profile(number_of, total, reach, slope), jnp.int32)
    pairs = (number_of - 1) // 2
    giver, receiver = lengths[1:1 + 2 * pairs:2], lengths[2:2 + 2 * pairs:2]
    room = jnp.minimum(giver - 1, reach - receiver)
    moved = jax.random.randint(jax.random.fold_in(own_key, 1), (pairs,), 0, 1 << 20) % (room + 1)
    lengths = lengths.at[1:1 + 2 * pairs:2].set(giver - moved).at[2:2 + 2 * pairs:2].set(receiver + moved)
    return lengths[jax.random.permutation(jax.random.fold_in(own_key, 2), number_of)]


def scatter_about(key, dims, scale, limit, cuts=(), kind=jnp.bfloat16):
    array = scale * jax.random.normal(key, dims, jnp.float32)
    if cuts:
        array = array * steps_of(key, dims, cuts, -0.22, 0.18)
    return jnp.clip(array, -limit, limit).astype(kind)


def setup_inputs(seed: int = 0) -> dict:
    splits = jax.random.split(jax.random.key(seed), 22)
    return {
        "tokens_in": scatter_about(splits[0], (SEQS, SEQ, D), 1.0, 6.0, ((0, 32),)),
        "cotangent": scatter_about(splits[1], (SEQS, SEQ, D), 1.0, 6.0, ((0, 32),)),
        "segment_ids": jax.vmap(lambda own: jnp.searchsorted(jnp.cumsum(ragged_sizes(own, DOCS, SEQ, DOC_MOST, 1)), jnp.arange(SEQ), side="right"))(jax.random.split(splits[2], SEQS)).reshape((SEQS, SEQ)).astype(jnp.int32),
        "in_weight": scatter_about(splits[3], (3, D, D), D ** -0.5, 0.1875, ((1, 32), (2, 4)), jnp.float32),
        "out_weight": scatter_about(splits[4], (D, D), D ** -0.5, 0.1875, ((0, 4), (1, 32)), jnp.float32),
        "gate_up_weight": scatter_about(splits[5], (2, D, FF), D ** -0.5, 0.1875, ((1, 32), (2, 4)), jnp.float32),
        "down_weight": scatter_about(splits[6], (FF, D), FF ** -0.5, 0.09375, ((0, 4), (1, 32)), jnp.float32),
        "conv_weight": scatter_about(splits[7], (TAPS, D), 0.6, 3.0, ((1, 4),), jnp.float32),
        "norm_gains": jnp.clip(1.0 + 0.1 * jax.random.normal(splits[8], (2, D), jnp.float32), 0.5, 1.5),
        "in_first": scatter_about(splits[9], (3, D, D), (0.11 * (SEQ * N_DP) ** 0.5), 84.48, ((1, 32), (2, 4)), jnp.float32),
        "in_second": jnp.clip(jnp.exp(math.log(3440.64) - 1.3843914 * jax.random.uniform(splits[10], (3, D, D), jnp.float32) ** steps_of(splits[10], (3, D, D), ((1, 32), (2, 4)), -0.2, 0.2)), 861.7984, 3440.64),
        "out_first": scatter_about(splits[11], (D, D), (0.14 * (SEQ * N_DP) ** 0.5), 107.52, ((0, 4), (1, 32)), jnp.float32),
        "out_second": jnp.clip(jnp.exp(math.log(5832.704) - 1.3862944 * jax.random.uniform(splits[12], (D, D), jnp.float32) ** steps_of(splits[12], (D, D), ((0, 4), (1, 32)), -0.2, 0.2)), 1458.176, 5832.704),
        "gate_up_first": scatter_about(splits[13], (2, D, FF), (0.033 * (SEQ * N_DP) ** 0.5), 25.6, ((1, 32), (2, 4)), jnp.float32),
        "gate_up_second": jnp.clip(jnp.exp(math.log(311.296) - 1.3968765 * jax.random.uniform(splits[14], (2, D, FF), jnp.float32) ** steps_of(splits[14], (2, D, FF), ((1, 32), (2, 4)), -0.2, 0.2)), 77.0048, 311.296),
        "down_first": scatter_about(splits[15], (FF, D), (0.055 * (SEQ * N_DP) ** 0.5), 42.24, ((0, 4), (1, 32)), jnp.float32),
        "down_second": jnp.clip(jnp.exp(math.log(851.968) - 1.3862944 * jax.random.uniform(splits[16], (FF, D), jnp.float32) ** steps_of(splits[16], (FF, D), ((0, 4), (1, 32)), -0.2, 0.2)), 212.992, 851.968),
        "conv_first": scatter_about(splits[17], (TAPS, D), (0.14 * (SEQ * N_DP) ** 0.5), 107.52, ((1, 4),), jnp.float32),
        "conv_second": jnp.clip(jnp.exp(math.log(5832.704) - 1.3862944 * jax.random.uniform(splits[18], (TAPS, D), jnp.float32) ** steps_of(splits[18], (TAPS, D), ((1, 4),), -0.2, 0.2)), 1458.176, 5832.704),
        "gains_first": scatter_about(splits[19], (2, D), (0.11 * (SEQ * N_DP) ** 0.5), 84.48, ((1, 32),), jnp.float32),
        "gains_second": jnp.clip(jnp.exp(math.log(3440.64) - 1.3843914 * jax.random.uniform(splits[20], (2, D), jnp.float32) ** steps_of(splits[20], (2, D), ((1, 32),), -0.2, 0.2)), 861.7984, 3440.64),
    }


@jax.custom_vjp
def low(v):
    return lax.optimization_barrier(v.astype(jnp.bfloat16)).astype(jnp.float32)

@jax.custom_vjp
def low_back(v):
    return v

def low_keep(v):
    return (low(v), None)

def low_pass(kept, grad):
    return (grad,)

def back_keep(v):
    return (v, None)

def back_low(kept, grad):
    return (low(grad),)
low.defvjp(low_keep, low_pass)
low_back.defvjp(back_keep, back_low)
highest = lax.Precision.HIGHEST
epsilon_norm = 1e-05
epsilon_adam = 1e-08
beta_one = 0.9
beta_two = 0.95

def rms_gain(values, gain_row):
    return values * lax.rsqrt(lax.optimization_barrier(jnp.mean(values * values, axis=-1, keepdims=True)) + epsilon_norm) * gain_row

def shifted(values, segments, offset):
    moved = jnp.concatenate([jnp.zeros((offset, values.shape[1]), values.dtype), values[:-offset]], axis=0)
    same = jnp.concatenate([jnp.zeros((offset,), jnp.bool_), segments[offset:] == segments[:-offset]])
    return jnp.where(same[:, None], moved, jnp.zeros_like(moved))

def forward(tokens, segments, in_weight, out_weight, gate_up_weight, down_weight, conv_weight, norm_gains):
    gains = low(norm_gains)
    normed_one = low(rms_gain(tokens, gains[0]))
    projected = low_back(jnp.einsum('td,kdc->ktc', normed_one, low(in_weight), precision=highest))
    product = projected[0] * projected[2]
    conv_sum = conv_weight[0] * product + conv_weight[1] * shifted(product, segments, 1)
    conv_sum = conv_sum + conv_weight[2] * shifted(product, segments, 2)
    gated = low(projected[1] * conv_sum)
    branch = low_back(jnp.dot(gated, low(out_weight), precision=highest))
    middle = tokens + branch
    normed_two = low(rms_gain(middle, gains[1]))
    gate_up = low_back(jnp.einsum('td,kdf->ktf', normed_two, low(gate_up_weight), precision=highest))
    hidden = low(jax.nn.silu(gate_up[0]) * gate_up[1])
    return middle + low_back(jnp.dot(hidden, low(down_weight), precision=highest))

def adam_step(master, gradient, first, second, step_rate, decay_rate):
    first_new = beta_one * first + (1.0 - beta_one) * gradient
    second_new = beta_two * second + (1.0 - beta_two) * gradient * gradient
    first_hat = first_new / (1.0 - beta_one ** ADAM_STEP)
    second_hat = second_new / (1.0 - beta_two ** ADAM_STEP)
    master_new = master - step_rate * (first_hat / (jnp.sqrt(second_hat) + epsilon_adam) + decay_rate * master)
    return (master_new, first_new, second_new)

def reference(tokens_in, cotangent, segment_ids, in_weight, out_weight, gate_up_weight, down_weight, conv_weight, norm_gains, in_first, in_second, out_first, out_second, gate_up_first, gate_up_second, down_first, down_second, conv_first, conv_second, gains_first, gains_second):
    params = (in_weight, out_weight, gate_up_weight, down_weight, conv_weight, norm_gains)

    def one_sequence(carry, item):
        tokens, back_out, segments = item

        def closed(values, *weights):
            return forward(values, segments, *weights)
        result, puller = jax.vjp(closed, tokens.astype(jnp.float32), *params)
        grads = puller(back_out.astype(jnp.float32))
        totals = tuple((total + grad for total, grad in zip(carry, grads[1:])))
        return (totals, (result, grads[0]))
    zeros = tuple((jnp.zeros_like(param) for param in params))
    sums, (results, tokens_grad) = lax.scan(one_sequence, zeros, (tokens_in, cotangent, segment_ids))
    rate_wide = 0.8 / D ** 0.5
    rate_down = 0.8 / FF ** 0.5
    in_new = adam_step(in_weight, sums[0], in_first, in_second, rate_wide, 0.1)
    out_new = adam_step(out_weight, sums[1], out_first, out_second, rate_wide, 0.1)
    gate_up_new = adam_step(gate_up_weight, sums[2], gate_up_first, gate_up_second, rate_wide, 0.1)
    down_new = adam_step(down_weight, sums[3], down_first, down_second, rate_down, 0.1)
    conv_new = adam_step(conv_weight, sums[4], conv_first, conv_second, 1.0, 0.0)
    gains_new = adam_step(norm_gains, sums[5], gains_first, gains_second, 0.3, 0.0)
    return (results, tokens_grad, in_new[0], in_new[1], in_new[2], out_new[0], out_new[1], out_new[2], gate_up_new[0], gate_up_new[1], gate_up_new[2], down_new[0], down_new[1], down_new[2], conv_new[0], conv_new[1], conv_new[2], gains_new[0], gains_new[1], gains_new[2])
```

```python
import jax
import jax.numpy as jnp
from jax import lax
from jax.sharding import PartitionSpec as P

D = 1024
FF = 4608
ADAM_STEP = 10
N_DP = 32
CORE_PAIRS = [(0, 1), (1, 0), (2, 3), (3, 2)]
HIGH_PAIRS = [(0, 2), (2, 0), (1, 3), (3, 1)]


epsilon_norm = 1e-05
epsilon_adam = 1e-08
beta_one = 0.9
beta_two = 0.95


def rms_gain(values, gain_row):
    return (
        values
        * lax.rsqrt(jnp.mean(values * values, axis=-1, keepdims=True) + epsilon_norm)
        * gain_row
    )


def adam_step(master, gradient, first, second, step_rate, decay_rate):
    first_new = beta_one * first + (1.0 - beta_one) * gradient
    second_new = beta_two * second + (1.0 - beta_two) * gradient * gradient
    first_hat = first_new / (1.0 - beta_one**ADAM_STEP)
    second_hat = second_new / (1.0 - beta_two**ADAM_STEP)
    master_new = master - step_rate * (
        first_hat / (jnp.sqrt(second_hat) + epsilon_adam) + decay_rate * master
    )
    return (master_new, first_new, second_new)


def spread(block):
    copies = jnp.broadcast_to(block[None], (N_DP,) + block.shape)
    return lax.all_to_all(copies, "dp", 0, 0, tiled=True).reshape(-1, block.shape[1])


def collect(grad):
    parts = grad.astype(jnp.bfloat16).reshape(N_DP, -1, grad.shape[1])
    parts = lax.all_to_all(parts, "dp", 0, 0, tiled=True)
    return jnp.sum(parts.astype(jnp.float32), axis=0)


def tensor_sum(part):
    core = lax.axis_index("tensor") % 2
    half = part.shape[0] // 2
    own = lax.dynamic_slice_in_dim(part, core * half, half, 0)
    other = lax.dynamic_slice_in_dim(part, (1 - core) * half, half, 0)
    pair = own + lax.ppermute(other, "tensor", CORE_PAIRS)
    pair = pair.astype(jnp.bfloat16)
    far = lax.ppermute(pair, "tensor", HIGH_PAIRS)
    total = pair.astype(jnp.float32) + far.astype(jnp.float32)
    twin = lax.ppermute(total, "tensor", CORE_PAIRS)
    first = core == 0
    return jnp.concatenate([jnp.where(first, total, twin), jnp.where(first, twin, total)], axis=0)


def shards(
    tokens_in,
    cotangent,
    segment_ids,
    in_weight,
    out_weight,
    gate_up_weight,
    down_weight,
    conv_weight,
    norm_gains,
    in_first,
    in_second,
    out_first,
    out_second,
    gate_up_first,
    gate_up_second,
    down_first,
    down_second,
    conv_first,
    conv_second,
    gains_first,
    gains_second,
):
    rows, length, width = tokens_in.shape
    count = rows * length
    taps_n, channels = conv_weight.shape
    units = gate_up_weight.shape[2]
    gains_full = lax.all_to_all(
        jnp.broadcast_to(norm_gains[None], (N_DP,) + norm_gains.shape), "dp", 0, 0, tiled=True
    )
    low_mix = jnp.concatenate(
        [in_weight[0], in_weight[1], in_weight[2], out_weight.T], axis=1
    ).astype(jnp.bfloat16)
    low_gate_up = jnp.concatenate([gate_up_weight[0], gate_up_weight[1]], axis=1).astype(
        jnp.bfloat16
    )
    low_down = down_weight.T.astype(jnp.bfloat16)
    mix_full = spread(low_mix)
    gate_up_full = spread(low_gate_up)
    down_full = spread(low_down)
    in_full = mix_full[:, : 3 * channels]
    out_full = mix_full[:, 3 * channels :]
    gains_value = (
        gains_full.transpose(1, 0, 2).reshape(2, width).astype(jnp.bfloat16).astype(jnp.float32)
    )
    flat = tokens_in.reshape(count, width).astype(jnp.float32)
    seg_flat = segment_ids.reshape(count)
    place = lax.iota(jnp.int32, count) % length
    mask_one = ((place >= 1) & (seg_flat == jnp.roll(seg_flat, 1)))[:, None]
    mask_two = ((place >= 2) & (seg_flat == jnp.roll(seg_flat, 2)))[:, None]

    def mixer_local(projected, taps):
        b_part = projected[:, :channels]
        c_part = projected[:, channels : 2 * channels]
        product = b_part * projected[:, 2 * channels :]
        conv_sum = taps[0] * product + taps[1] * jnp.where(
            mask_one, jnp.roll(product, 1, axis=0), 0.0
        )
        conv_sum = conv_sum + taps[2] * jnp.where(mask_two, jnp.roll(product, 2, axis=0), 0.0)
        return c_part * conv_sum

    def product_of(spec, left, right):
        return jnp.einsum(spec, left, right, preferred_element_type=jnp.float32)

    normed_one_f, norm_one_pull = jax.vjp(rms_gain, flat, gains_value[0])
    normed_one = normed_one_f.astype(jnp.bfloat16)
    projected = product_of("td,dc->tc", normed_one, in_full)
    gated_f, mixer_pull = jax.vjp(mixer_local, projected, conv_weight)
    gated = gated_f.astype(jnp.bfloat16)
    middle = flat + tensor_sum(product_of("tc,dc->td", gated, out_full))
    normed_two_f, norm_two_pull = jax.vjp(rms_gain, middle, gains_value[1])
    normed_two = normed_two_f.astype(jnp.bfloat16)
    gate_up = product_of("td,df->tf", normed_two, gate_up_full)

    def swish_gate(both):
        return jax.nn.silu(both[:, :units]) * both[:, units:]

    hidden_f, swish_pull = jax.vjp(swish_gate, gate_up)
    hidden = hidden_f.astype(jnp.bfloat16)
    back_out = cotangent.reshape(count, width)
    back_hidden = product_of("td,df->tf", back_out, down_full)
    back_gate_up = swish_pull(back_hidden)[0].astype(jnp.bfloat16)
    back_normed_two = tensor_sum(product_of("tf,df->td", back_gate_up, gate_up_full))
    red_down = collect(product_of("td,tf->df", back_out, hidden))
    red_gate_up = collect(product_of("td,tf->df", normed_two, back_gate_up))
    result = middle + tensor_sum(product_of("tf,df->td", hidden, down_full))
    back_middle_norm, grad_gain_two = norm_two_pull(back_normed_two)
    back_middle = back_out.astype(jnp.float32) + back_middle_norm
    back_branch = back_middle.astype(jnp.bfloat16)
    grad_out = product_of("td,tc->dc", back_branch, gated)
    back_gated = product_of("td,dc->tc", back_branch, out_full)
    back_projected_f, grad_conv = mixer_pull(back_gated)
    back_projected = back_projected_f.astype(jnp.bfloat16)
    grad_in = product_of("td,tc->dc", normed_one, back_projected)
    red_mix = collect(jnp.concatenate([grad_in, grad_out], axis=1))
    back_normed_one = tensor_sum(product_of("tc,dc->td", back_projected, in_full))
    back_tokens_norm, grad_gain_one = norm_one_pull(back_normed_one)
    back_tokens = back_middle + back_tokens_norm
    grad_gains = jnp.stack([grad_gain_one, grad_gain_two]).reshape(2, N_DP, -1).transpose(1, 0, 2)
    grad_small = jnp.concatenate(
        [
            grad_gains.reshape(N_DP, -1),
            jnp.broadcast_to(grad_conv.reshape(1, -1), (N_DP, grad_conv.size)),
        ],
        axis=1,
    )
    red_small = jnp.sum(lax.all_to_all(grad_small, "dp", 0, 0, tiled=True), axis=0)
    red_gains = red_small[: norm_gains.size].reshape(norm_gains.shape)
    conv_total = red_small[norm_gains.size :].reshape(conv_weight.shape)
    red_in = red_mix[:, : 3 * channels].reshape(-1, 3, channels).transpose(1, 0, 2)
    red_out = red_mix[:, 3 * channels :].T
    red_gate_up = red_gate_up.reshape(-1, 2, units).transpose(1, 0, 2)
    red_down = red_down.T
    rate_wide = 0.8 / D**0.5
    rate_down = 0.8 / FF**0.5
    in_new = adam_step(in_weight, red_in, in_first, in_second, rate_wide, 0.1)
    out_new = adam_step(out_weight, red_out, out_first, out_second, rate_wide, 0.1)
    gate_up_new = adam_step(
        gate_up_weight, red_gate_up, gate_up_first, gate_up_second, rate_wide, 0.1
    )
    down_new = adam_step(down_weight, red_down, down_first, down_second, rate_down, 0.1)
    conv_new = adam_step(conv_weight, conv_total, conv_first, conv_second, 1.0, 0.0)
    gains_new = adam_step(norm_gains, red_gains, gains_first, gains_second, 0.3, 0.0)
    return (
        result.reshape(rows, length, width),
        back_tokens.reshape(rows, length, width),
        in_new[0],
        in_new[1],
        in_new[2],
        out_new[0],
        out_new[1],
        out_new[2],
        gate_up_new[0],
        gate_up_new[1],
        gate_up_new[2],
        down_new[0],
        down_new[1],
        down_new[2],
        conv_new[0],
        conv_new[1],
        conv_new[2],
        gains_new[0],
        gains_new[1],
        gains_new[2],
    )


def solution(mesh):
    in_specs = (
        P("dp", None, None),
        P("dp", None, None),
        P("dp", None),
        P(None, "dp", "tensor"),
        P("tensor", "dp"),
        P(None, "dp", "tensor"),
        P("tensor", "dp"),
        P(None, "tensor"),
        P(None, "dp"),
        P(None, "dp", "tensor"),
        P(None, "dp", "tensor"),
        P("tensor", "dp"),
        P("tensor", "dp"),
        P(None, "dp", "tensor"),
        P(None, "dp", "tensor"),
        P("tensor", "dp"),
        P("tensor", "dp"),
        P(None, "tensor"),
        P(None, "tensor"),
        P(None, "dp"),
        P(None, "dp"),
    )
    out_specs = (
        P("dp", None, None),
        P("dp", None, None),
        P(None, "dp", "tensor"),
        P(None, "dp", "tensor"),
        P(None, "dp", "tensor"),
        P("tensor", "dp"),
        P("tensor", "dp"),
        P("tensor", "dp"),
        P(None, "dp", "tensor"),
        P(None, "dp", "tensor"),
        P(None, "dp", "tensor"),
        P("tensor", "dp"),
        P("tensor", "dp"),
        P("tensor", "dp"),
        P(None, "tensor"),
        P(None, "tensor"),
        P(None, "tensor"),
        P(None, "dp"),
        P(None, "dp"),
        P(None, "dp"),
    )
    return jax.shard_map(shards, mesh=mesh, in_specs=in_specs, out_specs=out_specs, check_vma=False)
```

```python
import jax
import jax.numpy as jnp
from jax import lax
from jax.experimental import pallas as pl
from jax.experimental.pallas import tpu as pltpu
from jax.sharding import PartitionSpec as P

D = 1024
FF = 4608
ADAM_STEP = 10
NX, NZ, NY = 4, 2, 4
N_DP = NX * NZ * NY
NEAR_PAIRS = [(d, d ^ NY) for d in range(N_DP)]
PLANES = [[(x * NZ + z) * NY + y for x in range(NX) for y in range(NY)] for z in range(NZ)]
CORE_PAIRS = [(0, 1), (1, 0), (2, 3), (3, 2)]
HIGH_PAIRS = [(0, 2), (2, 0), (1, 3), (3, 1)]


epsilon_norm = 1e-05
epsilon_adam = 1e-08
beta_one = 0.9
beta_two = 0.95


def rms_gain(values, gain_row):
    return (
        values
        * lax.rsqrt(jnp.mean(values * values, axis=-1, keepdims=True) + epsilon_norm)
        * gain_row
    )


def adam_step(master, gradient, first, second, step_rate, decay_rate):
    first_new = beta_one * first + (1.0 - beta_one) * gradient
    second_new = beta_two * second + (1.0 - beta_two) * gradient * gradient
    first_hat = first_new / (1.0 - beta_one**ADAM_STEP)
    second_hat = second_new / (1.0 - beta_two**ADAM_STEP)
    master_new = master - step_rate * (
        first_hat / (jnp.sqrt(second_hat) + epsilon_adam) + decay_rate * master
    )
    return (master_new, first_new, second_new)


def swap_core(value):
    return lax.ppermute(value, "tensor", CORE_PAIRS)


def swap_high(value):
    return lax.ppermute(value, "tensor", HIGH_PAIRS)


def swap_near(value):
    return lax.ppermute(value, "dp", NEAR_PAIRS)


def low(value):
    return value.astype(jnp.bfloat16)


def wide(value):
    return value.astype(jnp.float32)


def product_of(spec, left, right):
    return jnp.einsum(spec, left, right, preferred_element_type=jnp.float32)


def halves(value, core):
    half = value.shape[0] // 2
    return (
        lax.dynamic_slice_in_dim(value, core * half, half, 0),
        lax.dynamic_slice_in_dim(value, (1 - core) * half, half, 0),
    )


def joined(own, other, core):
    first = core == 0
    return jnp.concatenate([jnp.where(first, own, other), jnp.where(first, other, own)], axis=0)


def across_high(value):
    value = low(value)
    return wide(value) + wide(swap_high(value))


def sum_four(part, core):
    own, other = halves(part, core)
    return across_high(own + swap_core(other))


def sum_depth(pair):
    half = pair.shape[0] // 2
    return across_high(pair[:half] + wide(swap_near(low(pair[half:]))))


def to_planes(grad):
    columns = grad.shape[1]
    blocks = grad.reshape(NX, NZ, NY, -1, columns).transpose(0, 2, 1, 3, 4)
    return blocks.reshape(NX * NY, NZ, -1, columns)


def exchange(blocks):
    return lax.all_to_all(blocks, "dp", 0, 0, tiled=True, axis_index_groups=PLANES)


def in_order(mine, theirs, near):
    first = near == 0
    return jnp.where(first, mine, theirs), jnp.where(first, theirs, mine)


VMEM_BYTES = 40 * 1024 * 1024


def dot_rows(left, right):
    return lax.dot_general(left, right, (((1,), (1,)), ((), ())), preferred_element_type=jnp.float32)


def dot_columns(left, right):
    return lax.dot_general(left, right, (((0,), (0,)), ((), ())), preferred_element_type=jnp.float32)


def dot_plain(left, right):
    return jnp.dot(left, right, preferred_element_type=jnp.float32)


def hidden_kernel(
    normed_ref, back_ref, weights_ref, gate_ref, up_ref, hidden_ref, keep_ref, give_ref, held
):
    step = pl.program_id(0)
    rows = weights_ref.shape[3]

    @pl.when(step == 0)
    def _():
        for x in range(NX):
            for z in range(NZ):
                for y in range(NY):
                    start = ((x * NZ + z) * NY + y) * rows
                    for k in range(3):
                        held[k, start : start + rows, :] = weights_ref[x * NY + y, z, k]

    normed = normed_ref[...]
    gate = dot_plain(normed, held[0])
    up = dot_plain(normed, held[1])
    back = dot_plain(back_ref[...], held[2])
    share = jax.nn.sigmoid(gate)
    smooth = gate * share
    hidden_ref[...] = low(smooth * up)
    back_up = low(back * smooth)
    back_gate = low(back * up * (share + smooth * (1.0 - share)))
    gate_ref[...] = back_gate
    up_ref[...] = back_up
    part = dot_rows(back_gate, held[0]) + dot_rows(back_up, held[1])

    @pl.when(step < 2)
    def _():
        give_ref[...] = part

    @pl.when(step >= 2)
    def _():
        keep_ref[...] = part


def hidden_pass(normed, back, weights):
    tokens, width = normed.shape
    units = weights.shape[-1]
    block = tokens // 4
    turned = lambda i: ((i + 2) % 4, 0)
    narrow = jax.ShapeDtypeStruct((tokens, units), jnp.bfloat16)
    half = jax.ShapeDtypeStruct((tokens // 2, width), jnp.float32)
    return pl.pallas_call(
        hidden_kernel,
        grid=(4,),
        in_specs=[
            pl.BlockSpec((block, width), turned),
            pl.BlockSpec((block, width), turned),
            pl.BlockSpec(weights.shape, lambda i: (0, 0, 0, 0, 0)),
        ],
        out_specs=[
            pl.BlockSpec((block, units), turned),
            pl.BlockSpec((block, units), turned),
            pl.BlockSpec((block, units), turned),
            pl.BlockSpec((block, width), lambda i: (jnp.maximum(i - 2, 0), 0)),
            pl.BlockSpec((block, width), lambda i: (jnp.minimum(i, 1), 0)),
        ],
        out_shape=[narrow, narrow, narrow, half, half],
        scratch_shapes=[pltpu.VMEM((3, width, units), jnp.bfloat16)],
        compiler_params=pltpu.CompilerParams(vmem_limit_bytes=VMEM_BYTES),
        cost_estimate=pl.CostEstimate(
            flops=10 * tokens * width * units,
            bytes_accessed=16 * tokens * width,
            transcendentals=tokens * units,
        ),
        name="hidden_pass",
    )(normed, back, weights)


def grads_kernel(
    normed_ref, back_ref, gate_ref, up_ref, hidden_ref, down_ref, grads_ref, keep_ref, give_ref
):
    rows, units = down_ref.shape[3:]
    normed, back, hidden = normed_ref[...], back_ref[...], hidden_ref[...]
    for k, (left, right) in enumerate(
        ((normed, gate_ref[...]), (normed, up_ref[...]), (back, hidden))
    ):
        grad = low(dot_columns(left, right))
        for z in range(NZ):
            part = grad[z * NY * rows : (z + 1) * NY * rows]
            grads_ref[:, z, k] = part.reshape(NY, rows, units)
    down = jnp.concatenate(
        [down_ref[:, z, 0].reshape(NY * rows, units) for z in range(NZ)], axis=0
    )
    half = hidden.shape[0] // 2
    keep_ref[...] = dot_rows(hidden[:half], down)
    give_ref[...] = dot_rows(hidden[half:], down)


def grads_pass(normed, back, gate, up, hidden, weights):
    tokens, width = normed.shape
    units = weights.shape[-1]
    block = width // NX
    column = lambda i: (0, i)
    whole = lambda i: (0, 0)
    half = jax.ShapeDtypeStruct((tokens // 2, width), jnp.float32)
    return pl.pallas_call(
        grads_kernel,
        grid=(NX,),
        in_specs=[
            pl.BlockSpec((tokens, block), column),
            pl.BlockSpec((tokens, block), column),
            pl.BlockSpec((tokens, units), whole),
            pl.BlockSpec((tokens, units), whole),
            pl.BlockSpec((tokens, units), whole),
            pl.BlockSpec((NY, NZ, 1) + weights.shape[3:], lambda i: (i, 0, 2, 0, 0)),
        ],
        out_specs=[
            pl.BlockSpec((NY,) + weights.shape[1:], lambda i: (i, 0, 0, 0, 0)),
            pl.BlockSpec((tokens // 2, block), column),
            pl.BlockSpec((tokens // 2, block), column),
        ],
        out_shape=[jax.ShapeDtypeStruct(weights.shape, jnp.bfloat16), half, half],
        compiler_params=pltpu.CompilerParams(vmem_limit_bytes=VMEM_BYTES),
        cost_estimate=pl.CostEstimate(
            flops=8 * tokens * width * units,
            bytes_accessed=14 * tokens * width,
            transcendentals=0,
        ),
        name="grads_pass",
    )(normed, back, gate, up, hidden, weights)


def pieces(value):
    high = lax.reduce_precision(value, 8, 7)
    rest = value - high
    middle = lax.reduce_precision(rest, 8, 7)
    return [low(high), low(middle), low(rest - middle)]


def shards(
    tokens_in,
    cotangent,
    segment_ids,
    in_weight,
    out_weight,
    gate_up_weight,
    down_weight,
    conv_weight,
    norm_gains,
    in_first,
    in_second,
    out_first,
    out_second,
    gate_up_first,
    gate_up_second,
    down_first,
    down_second,
    conv_first,
    conv_second,
    gains_first,
    gains_second,
):
    rows, length, width = tokens_in.shape
    count = rows * length
    taps_n, channels = conv_weight.shape
    units = gate_up_weight.shape[2]
    own_rows = gate_up_weight.shape[1]
    part_units = units // NZ
    core = lax.axis_index("tensor") % 2
    near = (lax.axis_index("dp") // NY) % NZ

    mix_cols = 4 * channels
    low_mix = jnp.concatenate(
        [
            in_weight[0],
            in_weight[1],
            in_weight[2],
            out_weight.T,
            jnp.pad(norm_gains.T, ((0, 0), (0, 126))),
        ],
        axis=1,
    )
    low_mix = low(low_mix)
    low_ffn = low(jnp.concatenate([gate_up_weight, down_weight.T[None]], axis=0))
    keep = lax.dynamic_slice_in_dim(low_ffn, near * part_units, part_units, 2)
    give = lax.dynamic_slice_in_dim(low_ffn, (1 - near) * part_units, part_units, 2)
    take = swap_near(give)
    low_ffn = jnp.stack(in_order(keep, take, near), axis=0)
    ffn_copies = jnp.broadcast_to(low_ffn[None], (NX * NY,) + low_ffn.shape)
    back_out = cotangent.reshape(count, width)
    back_own, back_other = halves(back_out, core)
    back_near = swap_near(back_own)
    back_four = jnp.concatenate([back_own, back_near, back_other, swap_core(back_near)], axis=0)

    low_mix = jnp.stack(in_order(low_mix, swap_near(low_mix), near), axis=0)
    mix_full = exchange(jnp.broadcast_to(low_mix[None], (NX * NY,) + low_mix.shape))
    mix_full, ffn_copies, back_four = lax.optimization_barrier((mix_full, ffn_copies, back_four))
    ffn_full = exchange(ffn_copies)
    mix_full = mix_full.reshape(NX, NY, NZ, own_rows, -1).transpose(0, 2, 1, 3, 4).reshape(width, -1)
    in_full = mix_full[:, : 3 * channels]
    out_full = mix_full[:, 3 * channels : mix_cols]
    gains_value = wide(mix_full[:, mix_cols : mix_cols + 2]).T


    flat = wide(tokens_in.reshape(count, width))
    flat_half = halves(flat, core)[0]
    seg_flat = segment_ids.reshape(count)
    place = lax.iota(jnp.int32, count) % length
    mask_one = ((place >= 1) & (seg_flat == jnp.roll(seg_flat, 1)))[:, None]
    mask_two = ((place >= 2) & (seg_flat == jnp.roll(seg_flat, 2)))[:, None]

    def mixer_local(projected, taps):
        product = projected[:, :channels] * projected[:, 2 * channels :]
        conv_sum = taps[0] * product + taps[1] * jnp.where(
            mask_one, jnp.roll(product, 1, axis=0), 0.0
        )
        conv_sum = conv_sum + taps[2] * jnp.where(mask_two, jnp.roll(product, 2, axis=0), 0.0)
        return projected[:, channels : 2 * channels] * conv_sum

    normed_one = low(rms_gain(flat, gains_value[0]))
    projected = product_of("td,dc->tc", normed_one, in_full)
    gated_f, mixer_pull = jax.vjp(mixer_local, projected, conv_weight)
    gated = low(gated_f)
    middle = flat_half + sum_four(product_of("tc,dc->td", gated, out_full), core)
    normed_two_f, norm_two_pull = jax.vjp(rms_gain, middle, gains_value[1])
    normed_two = low(normed_two_f)
    normed_two = jnp.concatenate([normed_two, swap_near(normed_two)], axis=0)
    normed_two = jnp.concatenate([normed_two, swap_core(normed_two)], axis=0)

    back_gate, back_up, hidden, back_keep, back_give = hidden_pass(
        normed_two, back_four, ffn_full
    )
    back_pair = back_keep + swap_core(back_give)
    back_pair, back_gate, back_up, hidden = lax.optimization_barrier(
        (back_pair, back_gate, back_up, hidden)
    )
    back_normed_two = sum_depth(back_pair)
    grad_ffn, ffn_keep, ffn_give = grads_pass(
        normed_two, back_four, back_gate, back_up, hidden, ffn_full
    )
    grad_ffn = exchange(grad_ffn)

    ffn_keep, ffn_give, back_normed_two = lax.optimization_barrier(
        (ffn_keep, ffn_give, back_normed_two)
    )
    result = middle + sum_depth(ffn_keep + swap_core(ffn_give))
    result = joined(result, swap_core(result), core)

    back_middle_norm, grad_gain_two = norm_two_pull(back_normed_two)
    back_middle = wide(back_own) + back_middle_norm
    back_branch = low(back_middle)
    back_branch = joined(back_branch, swap_core(back_branch), core)
    grad_out = product_of("td,tc->dc", back_branch, gated)
    back_gated = product_of("td,dc->tc", back_branch, out_full)
    back_projected_f, grad_conv = mixer_pull(back_gated)
    back_projected = low(back_projected_f)
    grad_in = product_of("td,tc->dc", normed_one, back_projected)
    back_normed_one = product_of("tc,dc->td", back_projected, in_full)
    grad_gain_one = jnp.sum(back_normed_one * rms_gain(flat, 1.0), axis=0)
    grad_gains = jnp.stack([grad_gain_one, 0.5 * grad_gain_two])
    grad_gains = grad_gains.reshape(2, N_DP, own_rows).transpose(1, 0, 2).reshape(N_DP, -1)
    grad_conv = jnp.broadcast_to(grad_conv.reshape(1, -1), (N_DP, grad_conv.size))
    small_size = grad_gains.shape[1] + grad_conv.shape[1]
    small = jnp.concatenate([grad_gains, grad_conv], axis=1)
    small = jnp.pad(small, ((0, 0), (0, 1024 - small_size))).reshape(N_DP, 8, 128)
    small = jnp.concatenate(pieces(small) + [jnp.zeros((N_DP, own_rows - 24, 128), jnp.bfloat16)], axis=1)
    grad_mix = jnp.concatenate([low(grad_in), low(grad_out), small.reshape(width, 128)], axis=1)
    grad_mix = to_planes(grad_mix)
    grad_ffn, grad_mix = lax.optimization_barrier((grad_ffn, grad_mix))
    red_mix = jnp.sum(wide(exchange(grad_mix)), axis=0)
    keep = lax.dynamic_index_in_dim(red_mix, near, 0, keepdims=False)
    red_mix = keep + swap_near(lax.dynamic_index_in_dim(red_mix, 1 - near, 0, keepdims=False))
    grad_ffn = jnp.sum(wide(grad_ffn), axis=0)
    keep = lax.dynamic_index_in_dim(grad_ffn, near, 0, keepdims=False)
    take = swap_near(lax.dynamic_index_in_dim(grad_ffn, 1 - near, 0, keepdims=False))
    red_ffn = jnp.concatenate(in_order(keep, take, near), axis=2)
    back_normed_one = sum_four(back_normed_one, core)
    back_tokens_norm = jax.vjp(rms_gain, flat_half, gains_value[0])[1](back_normed_one)[0]
    back_tokens = back_middle + back_tokens_norm
    back_tokens = joined(back_tokens, swap_core(back_tokens), core)

    red_small = jnp.sum(red_mix[:24, mix_cols:].reshape(3, 1024), axis=0)
    red_gains = red_small[: norm_gains.size].reshape(norm_gains.shape)
    twin_gains = swap_core(red_gains)
    high_gains = swap_high(red_gains) + swap_high(twin_gains)
    red_gains = (red_gains + twin_gains) + high_gains
    conv_total = red_small[norm_gains.size : small_size].reshape(conv_weight.shape)
    red_in = red_mix[:, : 3 * channels].reshape(-1, 3, channels).transpose(1, 0, 2)
    red_out = red_mix[:, 3 * channels : mix_cols].T
    red_gate_up = red_ffn[:2]
    red_down = red_ffn[2].T
    rate_wide = 0.8 / D**0.5
    rate_down = 0.8 / FF**0.5
    in_new = adam_step(in_weight, red_in, in_first, in_second, rate_wide, 0.1)
    out_new = adam_step(out_weight, red_out, out_first, out_second, rate_wide, 0.1)
    gate_up_new = adam_step(
        gate_up_weight, red_gate_up, gate_up_first, gate_up_second, rate_wide, 0.1
    )
    down_new = adam_step(down_weight, red_down, down_first, down_second, rate_down, 0.1)
    conv_new = adam_step(conv_weight, conv_total, conv_first, conv_second, 1.0, 0.0)
    gains_new = adam_step(norm_gains, red_gains, gains_first, gains_second, 0.3, 0.0)
    return (
        result.reshape(rows, length, width),
        back_tokens.reshape(rows, length, width),
        in_new[0],
        in_new[1],
        in_new[2],
        out_new[0],
        out_new[1],
        out_new[2],
        gate_up_new[0],
        gate_up_new[1],
        gate_up_new[2],
        down_new[0],
        down_new[1],
        down_new[2],
        conv_new[0],
        conv_new[1],
        conv_new[2],
        gains_new[0],
        gains_new[1],
        gains_new[2],
    )


def solution(mesh):
    in_specs = (
        P("dp", None, None),
        P("dp", None, None),
        P("dp", None),
        P(None, "dp", "tensor"),
        P("tensor", "dp"),
        P(None, "dp", "tensor"),
        P("tensor", "dp"),
        P(None, "tensor"),
        P(None, "dp"),
        P(None, "dp", "tensor"),
        P(None, "dp", "tensor"),
        P("tensor", "dp"),
        P("tensor", "dp"),
        P(None, "dp", "tensor"),
        P(None, "dp", "tensor"),
        P("tensor", "dp"),
        P("tensor", "dp"),
        P(None, "tensor"),
        P(None, "tensor"),
        P(None, "dp"),
        P(None, "dp"),
    )
    out_specs = (
        P("dp", None, None),
        P("dp", None, None),
        P(None, "dp", "tensor"),
        P(None, "dp", "tensor"),
        P(None, "dp", "tensor"),
        P("tensor", "dp"),
        P("tensor", "dp"),
        P("tensor", "dp"),
        P(None, "dp", "tensor"),
        P(None, "dp", "tensor"),
        P(None, "dp", "tensor"),
        P("tensor", "dp"),
        P("tensor", "dp"),
        P("tensor", "dp"),
        P(None, "tensor"),
        P(None, "tensor"),
        P(None, "tensor"),
        P(None, "dp"),
        P(None, "dp"),
        P(None, "dp"),
    )
    return jax.shard_map(shards, mesh=mesh, in_specs=in_specs, out_specs=out_specs, check_vma=False)
```

```python
import jax
import jax.numpy as jnp
from jax import lax
from jax.experimental import pallas as pl
from jax.experimental.pallas import tpu as pltpu
from jax.sharding import PartitionSpec as P

D = 1024
FF = 4608
ADAM_STEP = 10
NX, NZ, NY = 4, 2, 4
N_DP = NX * NZ * NY
NEAR_PAIRS = [(d, d ^ NY) for d in range(N_DP)]
PLANES = [[(x * NZ + z) * NY + y for x in range(NX) for y in range(NY)] for z in range(NZ)]
CORE_PAIRS = [(0, 1), (1, 0), (2, 3), (3, 2)]
HIGH_PAIRS = [(0, 2), (2, 0), (1, 3), (3, 1)]


epsilon_norm = 1e-05
epsilon_adam = 1e-08
beta_one = 0.9
beta_two = 0.95


def rms_gain(values, gain_row):
    return (
        values
        * lax.rsqrt(jnp.mean(values * values, axis=-1, keepdims=True) + epsilon_norm)
        * gain_row
    )


def adam_step(master, gradient, first, second, step_rate, decay_rate):
    first_new = beta_one * first + (1.0 - beta_one) * gradient
    second_new = beta_two * second + (1.0 - beta_two) * gradient * gradient
    first_hat = first_new / (1.0 - beta_one**ADAM_STEP)
    second_hat = second_new / (1.0 - beta_two**ADAM_STEP)
    master_new = master - step_rate * (
        first_hat / (jnp.sqrt(second_hat) + epsilon_adam) + decay_rate * master
    )
    return (master_new, first_new, second_new)


def swap_core(value):
    return lax.ppermute(value, "tensor", CORE_PAIRS)


def swap_high(value):
    return lax.ppermute(value, "tensor", HIGH_PAIRS)


def swap_near(value):
    return lax.ppermute(value, "dp", NEAR_PAIRS)


def low(value):
    return value.astype(jnp.bfloat16)


def wide(value):
    return value.astype(jnp.float32)


def product_of(spec, left, right):
    return jnp.einsum(spec, left, right, preferred_element_type=jnp.float32)


def halves(value, core):
    half = value.shape[0] // 2
    return (
        lax.dynamic_slice_in_dim(value, core * half, half, 0),
        lax.dynamic_slice_in_dim(value, (1 - core) * half, half, 0),
    )


def joined(own, other, core):
    first = core == 0
    return jnp.concatenate([jnp.where(first, own, other), jnp.where(first, other, own)], axis=0)


def across_high(value):
    value = low(value)
    return wide(value) + wide(swap_high(value))


def sum_four(part, core):
    own, other = halves(part, core)
    return across_high(own + swap_core(other))


def sum_depth(pair):
    half = pair.shape[0] // 2
    return across_high(pair[:half] + wide(swap_near(low(pair[half:]))))


def to_planes(grad):
    columns = grad.shape[1]
    blocks = grad.reshape(NX, NZ, NY, -1, columns).transpose(0, 2, 1, 3, 4)
    return blocks.reshape(NX * NY, NZ, -1, columns)


def exchange(blocks):
    return lax.all_to_all(blocks, "dp", 0, 0, tiled=True, axis_index_groups=PLANES)


def in_order(mine, theirs, near):
    first = near == 0
    return jnp.where(first, mine, theirs), jnp.where(first, theirs, mine)


def whole_units(grad, near):
    keep = lax.dynamic_index_in_dim(grad, near, 0, keepdims=False)
    take = swap_near(lax.dynamic_index_in_dim(grad, 1 - near, 0, keepdims=False))
    return jnp.concatenate(in_order(keep, take, near), axis=-1)


VMEM_BYTES = 40 * 1024 * 1024


def dot_rows(left, right):
    return lax.dot_general(left, right, (((1,), (1,)), ((), ())), preferred_element_type=jnp.float32)


def dot_columns(left, right):
    return lax.dot_general(left, right, (((0,), (0,)), ((), ())), preferred_element_type=jnp.float32)


def dot_plain(left, right):
    return jnp.dot(left, right, preferred_element_type=jnp.float32)


def hidden_kernel(
    normed_ref, back_ref, weights_ref, gate_ref, up_ref, hidden_ref, keep_ref, give_ref, held
):
    step = pl.program_id(0)
    rows = weights_ref.shape[3]

    @pl.when(step == 0)
    def _():
        for x in range(NX):
            for z in range(NZ):
                for y in range(NY):
                    start = ((x * NZ + z) * NY + y) * rows
                    for k in range(3):
                        held[k, start : start + rows, :] = weights_ref[x * NY + y, z, k]

    normed = normed_ref[...]
    gate = dot_plain(normed, held[0])
    up = dot_plain(normed, held[1])
    back = dot_plain(back_ref[...], held[2])
    share = jax.nn.sigmoid(gate)
    smooth = gate * share
    hidden_ref[...] = low(smooth * up)
    back_up = low(back * smooth)
    back_gate = low(back * up * (share + smooth * (1.0 - share)))
    gate_ref[...] = back_gate
    up_ref[...] = back_up
    part = dot_rows(back_gate, held[0]) + dot_rows(back_up, held[1])

    @pl.when(step < 2)
    def _():
        give_ref[...] = part

    @pl.when(step >= 2)
    def _():
        keep_ref[...] = part


def hidden_pass(normed, back, weights):
    tokens, width = normed.shape
    units = weights.shape[-1]
    block = tokens // 4
    turned = lambda i: ((i + 2) % 4, 0)
    narrow = jax.ShapeDtypeStruct((tokens, units), jnp.bfloat16)
    half = jax.ShapeDtypeStruct((tokens // 2, width), jnp.float32)
    return pl.pallas_call(
        hidden_kernel,
        grid=(4,),
        in_specs=[
            pl.BlockSpec((block, width), turned),
            pl.BlockSpec((block, width), turned),
            pl.BlockSpec(weights.shape, lambda i: (0, 0, 0, 0, 0)),
        ],
        out_specs=[
            pl.BlockSpec((block, units), turned),
            pl.BlockSpec((block, units), turned),
            pl.BlockSpec((block, units), turned),
            pl.BlockSpec((block, width), lambda i: (jnp.maximum(i - 2, 0), 0)),
            pl.BlockSpec((block, width), lambda i: (jnp.minimum(i, 1), 0)),
        ],
        out_shape=[narrow, narrow, narrow, half, half],
        scratch_shapes=[pltpu.VMEM((3, width, units), jnp.bfloat16)],
        compiler_params=pltpu.CompilerParams(vmem_limit_bytes=VMEM_BYTES),
        cost_estimate=pl.CostEstimate(
            flops=10 * tokens * width * units,
            bytes_accessed=16 * tokens * width,
            transcendentals=tokens * units,
        ),
        name="hidden_pass",
    )(normed, back, weights)


def grads_kernel(
    normed_ref,
    back_ref,
    gate_ref,
    up_ref,
    hidden_ref,
    down_ref,
    pair_grad_ref,
    down_grad_ref,
    keep_ref,
    give_ref,
):
    rows, units = down_ref.shape[3:]
    plane = NY * rows
    normed, hidden = normed_ref[...], hidden_ref[...]
    for k, right in enumerate((gate_ref[...], up_ref[...])):
        grad = low(dot_columns(normed, right))
        for z in range(NZ):
            part = grad[z * plane : (z + 1) * plane]
            pair_grad_ref[:, z, k] = part.reshape(NY, rows, units)
    grad = low(dot_columns(back_ref[...], hidden))
    for z in range(NZ):
        down_grad_ref[:, z] = grad[z * plane : (z + 1) * plane].reshape(NY, rows, units)
    down = jnp.concatenate(
        [down_ref[:, z, 0].reshape(plane, units) for z in range(NZ)], axis=0
    )
    half = hidden.shape[0] // 2
    keep_ref[...] = dot_rows(hidden[:half], down)
    give_ref[...] = dot_rows(hidden[half:], down)


def grads_pass(normed, back, gate, up, hidden, weights):
    tokens, width = normed.shape
    rows, units = weights.shape[3:]
    block = width // NX
    column = lambda i: (0, i)
    whole = lambda i: (0, 0)
    half = jax.ShapeDtypeStruct((tokens // 2, width), jnp.float32)
    return pl.pallas_call(
        grads_kernel,
        grid=(NX,),
        in_specs=[
            pl.BlockSpec((tokens, block), column),
            pl.BlockSpec((tokens, block), column),
            pl.BlockSpec((tokens, units), whole),
            pl.BlockSpec((tokens, units), whole),
            pl.BlockSpec((tokens, units), whole),
            pl.BlockSpec((NY, NZ, 1, rows, units), lambda i: (i, 0, 2, 0, 0)),
        ],
        out_specs=[
            pl.BlockSpec((NY, NZ, 2, rows, units), lambda i: (i, 0, 0, 0, 0)),
            pl.BlockSpec((NY, NZ, rows, units), lambda i: (i, 0, 0, 0)),
            pl.BlockSpec((tokens // 2, block), column),
            pl.BlockSpec((tokens // 2, block), column),
        ],
        out_shape=[
            jax.ShapeDtypeStruct((NX * NY, NZ, 2, rows, units), jnp.bfloat16),
            jax.ShapeDtypeStruct((NX * NY, NZ, rows, units), jnp.bfloat16),
            half,
            half,
        ],
        compiler_params=pltpu.CompilerParams(vmem_limit_bytes=VMEM_BYTES),
        cost_estimate=pl.CostEstimate(
            flops=8 * tokens * width * units,
            bytes_accessed=14 * tokens * width,
            transcendentals=0,
        ),
        name="grads_pass",
    )(normed, back, gate, up, hidden, weights)


def pieces(value):
    high = lax.reduce_precision(value, 8, 7)
    rest = value - high
    middle = lax.reduce_precision(rest, 8, 7)
    return [low(high), low(middle), low(rest - middle)]


def shards(
    tokens_in,
    cotangent,
    segment_ids,
    in_weight,
    out_weight,
    gate_up_weight,
    down_weight,
    conv_weight,
    norm_gains,
    in_first,
    in_second,
    out_first,
    out_second,
    gate_up_first,
    gate_up_second,
    down_first,
    down_second,
    conv_first,
    conv_second,
    gains_first,
    gains_second,
):
    rows, length, width = tokens_in.shape
    count = rows * length
    taps_n, channels = conv_weight.shape
    units = gate_up_weight.shape[2]
    own_rows = gate_up_weight.shape[1]
    part_units = units // NZ
    core = lax.axis_index("tensor") % 2
    near = (lax.axis_index("dp") // NY) % NZ

    mix_cols = 4 * channels
    low_mix = jnp.concatenate(
        [
            in_weight[0],
            in_weight[1],
            in_weight[2],
            out_weight.T,
            jnp.pad(norm_gains.T, ((0, 0), (0, 126))),
        ],
        axis=1,
    )
    low_mix = low(low_mix)
    low_ffn = low(jnp.concatenate([gate_up_weight, down_weight.T[None]], axis=0))
    keep = lax.dynamic_slice_in_dim(low_ffn, near * part_units, part_units, 2)
    give = lax.dynamic_slice_in_dim(low_ffn, (1 - near) * part_units, part_units, 2)
    take = swap_near(give)
    low_ffn = jnp.stack(in_order(keep, take, near), axis=0)
    ffn_copies = jnp.broadcast_to(low_ffn[None], (NX * NY,) + low_ffn.shape)
    back_out = cotangent.reshape(count, width)
    back_own, back_other = halves(back_out, core)
    back_near = swap_near(back_own)
    back_four = jnp.concatenate([back_own, back_near, back_other, swap_core(back_near)], axis=0)

    low_mix = jnp.stack(in_order(low_mix, swap_near(low_mix), near), axis=0)
    mix_full = exchange(jnp.broadcast_to(low_mix[None], (NX * NY,) + low_mix.shape))
    mix_full, ffn_copies, back_four = lax.optimization_barrier((mix_full, ffn_copies, back_four))
    ffn_full = exchange(ffn_copies)
    mix_full = mix_full.reshape(NX, NY, NZ, own_rows, -1).transpose(0, 2, 1, 3, 4).reshape(width, -1)
    in_full = mix_full[:, : 3 * channels]
    out_full = mix_full[:, 3 * channels : mix_cols]
    gains_value = wide(mix_full[:, mix_cols : mix_cols + 2]).T


    flat = wide(tokens_in.reshape(count, width))
    flat_half = halves(flat, core)[0]
    seg_flat = segment_ids.reshape(count)
    place = lax.iota(jnp.int32, count) % length
    mask_one = ((place >= 1) & (seg_flat == jnp.roll(seg_flat, 1)))[:, None]
    mask_two = ((place >= 2) & (seg_flat == jnp.roll(seg_flat, 2)))[:, None]

    def mixer_local(projected, taps):
        product = projected[:, :channels] * projected[:, 2 * channels :]
        conv_sum = taps[0] * product + taps[1] * jnp.where(
            mask_one, jnp.roll(product, 1, axis=0), 0.0
        )
        conv_sum = conv_sum + taps[2] * jnp.where(mask_two, jnp.roll(product, 2, axis=0), 0.0)
        return projected[:, channels : 2 * channels] * conv_sum

    normed_one = low(rms_gain(flat, gains_value[0]))
    projected = product_of("td,dc->tc", normed_one, in_full)
    gated_f, mixer_pull = jax.vjp(mixer_local, projected, conv_weight)
    gated = low(gated_f)
    middle = flat_half + sum_four(product_of("tc,dc->td", gated, out_full), core)
    normed_two_f, norm_two_pull = jax.vjp(rms_gain, middle, gains_value[1])
    normed_two = low(normed_two_f)
    normed_two = jnp.concatenate([normed_two, swap_near(normed_two)], axis=0)
    normed_two, ffn_full = lax.optimization_barrier((normed_two, ffn_full))
    normed_two = jnp.concatenate([normed_two, swap_core(normed_two)], axis=0)

    back_gate, back_up, hidden, back_keep, back_give = hidden_pass(
        normed_two, back_four, ffn_full
    )
    grad_pair, grad_down, ffn_keep, ffn_give = grads_pass(
        normed_two, back_four, back_gate, back_up, hidden, ffn_full
    )
    back_pair = back_keep + swap_core(back_give)
    back_pair, grad_down = lax.optimization_barrier((back_pair, grad_down))
    back_normed_two = sum_depth(back_pair)
    grad_down = exchange(grad_down)
    back_normed_two, grad_down, grad_pair = lax.optimization_barrier(
        (back_normed_two, grad_down, grad_pair)
    )
    grad_pair = exchange(grad_pair)
    ffn_keep, ffn_give, back_normed_two = lax.optimization_barrier(
        (ffn_keep, ffn_give, back_normed_two)
    )
    result = middle + sum_depth(ffn_keep + swap_core(ffn_give))
    result = joined(result, swap_core(result), core)

    back_middle_norm, grad_gain_two = norm_two_pull(back_normed_two)
    back_middle = wide(back_own) + back_middle_norm
    back_branch = low(back_middle)
    back_branch = joined(back_branch, swap_core(back_branch), core)
    grad_out = product_of("td,tc->dc", back_branch, gated)
    back_gated = product_of("td,dc->tc", back_branch, out_full)
    back_projected_f, grad_conv = mixer_pull(back_gated)
    back_projected = low(back_projected_f)
    grad_in = product_of("td,tc->dc", normed_one, back_projected)
    back_normed_one = product_of("tc,dc->td", back_projected, in_full)
    grad_gain_one = jnp.sum(back_normed_one * rms_gain(flat, 1.0), axis=0)
    grad_gains = jnp.stack([grad_gain_one, 0.5 * grad_gain_two])
    grad_gains = grad_gains + swap_core(grad_gains)
    grad_gains = grad_gains + swap_high(grad_gains)
    grad_gains = grad_gains.reshape(2, N_DP, own_rows).transpose(1, 0, 2).reshape(N_DP, -1)
    grad_conv = jnp.broadcast_to(grad_conv.reshape(1, -1), (N_DP, grad_conv.size))
    small_size = grad_gains.shape[1] + grad_conv.shape[1]
    small = jnp.concatenate([grad_gains, grad_conv], axis=1)
    small = jnp.pad(small, ((0, 0), (0, 1024 - small_size))).reshape(N_DP, 8, 128)
    small = jnp.concatenate(pieces(small) + [jnp.zeros((N_DP, own_rows - 24, 128), jnp.bfloat16)], axis=1)
    grad_mix = jnp.concatenate([low(grad_in), low(grad_out), small.reshape(width, 128)], axis=1)
    grad_mix = to_planes(grad_mix)
    grad_pair, grad_mix = lax.optimization_barrier((grad_pair, grad_mix))
    red_mix = jnp.sum(wide(exchange(grad_mix)), axis=0)
    keep = lax.dynamic_index_in_dim(red_mix, near, 0, keepdims=False)
    red_mix = keep + swap_near(lax.dynamic_index_in_dim(red_mix, 1 - near, 0, keepdims=False))
    red_down = whole_units(jnp.sum(wide(grad_down), axis=0), near).T
    red_gate_up = whole_units(jnp.sum(wide(grad_pair), axis=0), near)
    back_normed_one = sum_four(back_normed_one, core)
    back_tokens_norm = jax.vjp(rms_gain, flat_half, gains_value[0])[1](back_normed_one)[0]
    back_tokens = back_middle + back_tokens_norm
    back_tokens = joined(back_tokens, swap_core(back_tokens), core)

    red_small = jnp.sum(red_mix[:24, mix_cols:].reshape(3, 1024), axis=0)
    red_gains = red_small[: norm_gains.size].reshape(norm_gains.shape)
    conv_total = red_small[norm_gains.size : small_size].reshape(conv_weight.shape)
    red_in = red_mix[:, : 3 * channels].reshape(-1, 3, channels).transpose(1, 0, 2)
    red_out = red_mix[:, 3 * channels : mix_cols].T
    rate_wide = 0.8 / D**0.5
    rate_down = 0.8 / FF**0.5
    in_new = adam_step(in_weight, red_in, in_first, in_second, rate_wide, 0.1)
    out_new = adam_step(out_weight, red_out, out_first, out_second, rate_wide, 0.1)
    gate_up_new = adam_step(
        gate_up_weight, red_gate_up, gate_up_first, gate_up_second, rate_wide, 0.1
    )
    down_new = adam_step(down_weight, red_down, down_first, down_second, rate_down, 0.1)
    conv_new = adam_step(conv_weight, conv_total, conv_first, conv_second, 1.0, 0.0)
    gains_new = adam_step(norm_gains, red_gains, gains_first, gains_second, 0.3, 0.0)
    return (
        result.reshape(rows, length, width),
        back_tokens.reshape(rows, length, width),
        in_new[0],
        in_new[1],
        in_new[2],
        out_new[0],
        out_new[1],
        out_new[2],
        gate_up_new[0],
        gate_up_new[1],
        gate_up_new[2],
        down_new[0],
        down_new[1],
        down_new[2],
        conv_new[0],
        conv_new[1],
        conv_new[2],
        gains_new[0],
        gains_new[1],
        gains_new[2],
    )


def solution(mesh):
    in_specs = (
        P("dp", None, None),
        P("dp", None, None),
        P("dp", None),
        P(None, "dp", "tensor"),
        P("tensor", "dp"),
        P(None, "dp", "tensor"),
        P("tensor", "dp"),
        P(None, "tensor"),
        P(None, "dp"),
        P(None, "dp", "tensor"),
        P(None, "dp", "tensor"),
        P("tensor", "dp"),
        P("tensor", "dp"),
        P(None, "dp", "tensor"),
        P(None, "dp", "tensor"),
        P("tensor", "dp"),
        P("tensor", "dp"),
        P(None, "tensor"),
        P(None, "tensor"),
        P(None, "dp"),
        P(None, "dp"),
    )
    out_specs = (
        P("dp", None, None),
        P("dp", None, None),
        P(None, "dp", "tensor"),
        P(None, "dp", "tensor"),
        P(None, "dp", "tensor"),
        P("tensor", "dp"),
        P("tensor", "dp"),
        P("tensor", "dp"),
        P(None, "dp", "tensor"),
        P(None, "dp", "tensor"),
        P(None, "dp", "tensor"),
        P("tensor", "dp"),
        P("tensor", "dp"),
        P("tensor", "dp"),
        P(None, "tensor"),
        P(None, "tensor"),
        P(None, "tensor"),
        P(None, "dp"),
        P(None, "dp"),
        P(None, "dp"),
    )
    return jax.shard_map(shards, mesh=mesh, in_specs=in_specs, out_specs=out_specs, check_vma=False)
```

```python
import jax
import jax.numpy as jnp
from jax import lax
from jax.experimental import pallas as pl
from jax.experimental.pallas import tpu as pltpu
from jax.sharding import PartitionSpec as P

D = 1024
FF = 4608
ADAM_STEP = 10
NX, NZ, NY = 4, 2, 4
N_DP = NX * NZ * NY
NEAR_PAIRS = [(d, d ^ NY) for d in range(N_DP)]
PLANES = [[(x * NZ + z) * NY + y for x in range(NX) for y in range(NY)] for z in range(NZ)]
CORE_PAIRS = [(0, 1), (1, 0), (2, 3), (3, 2)]
HIGH_PAIRS = [(0, 2), (2, 0), (1, 3), (3, 1)]


epsilon_norm = 1e-05
epsilon_adam = 1e-08
beta_one = 0.9
beta_two = 0.95


def rms_gain(values, gain_row):
    return (
        values
        * lax.rsqrt(jnp.mean(values * values, axis=-1, keepdims=True) + epsilon_norm)
        * gain_row
    )


def adam_step(master, gradient, first, second, step_rate, decay_rate):
    first_new = beta_one * first + (1.0 - beta_one) * gradient
    second_new = beta_two * second + (1.0 - beta_two) * gradient * gradient
    first_hat = first_new / (1.0 - beta_one**ADAM_STEP)
    second_hat = second_new / (1.0 - beta_two**ADAM_STEP)
    master_new = master - step_rate * (
        first_hat / (jnp.sqrt(second_hat) + epsilon_adam) + decay_rate * master
    )
    return (master_new, first_new, second_new)


def swap_core(value):
    return lax.ppermute(value, "tensor", CORE_PAIRS)


def swap_high(value):
    return lax.ppermute(value, "tensor", HIGH_PAIRS)


def swap_near(value):
    return lax.ppermute(value, "dp", NEAR_PAIRS)


def low(value):
    return value.astype(jnp.bfloat16)


def wide(value):
    return value.astype(jnp.float32)


def product_of(spec, left, right):
    return jnp.einsum(spec, left, right, preferred_element_type=jnp.float32)


def halves(value, core):
    half = value.shape[0] // 2
    return (
        lax.dynamic_slice_in_dim(value, core * half, half, 0),
        lax.dynamic_slice_in_dim(value, (1 - core) * half, half, 0),
    )


def joined(own, other, core):
    first = core == 0
    return jnp.concatenate([jnp.where(first, own, other), jnp.where(first, other, own)], axis=0)


def across_high(value):
    value = low(value)
    return wide(value) + wide(swap_high(value))


def sum_four(part, core):
    own, other = halves(part, core)
    return across_high(own + swap_core(other))


def to_planes(grad):
    columns = grad.shape[1]
    blocks = grad.reshape(NX, NZ, NY, -1, columns).transpose(0, 2, 1, 3, 4)
    return blocks.reshape(NX * NY, NZ, -1, columns)


def exchange(blocks):
    return lax.all_to_all(blocks, "dp", 0, 0, tiled=True, axis_index_groups=PLANES)


def in_order(mine, theirs, near):
    first = near == 0
    return jnp.where(first, mine, theirs), jnp.where(first, theirs, mine)


def whole_units(grad, near):
    keep = lax.dynamic_index_in_dim(grad, near, 0, keepdims=False)
    take = swap_near(lax.dynamic_index_in_dim(grad, 1 - near, 0, keepdims=False))
    return jnp.concatenate(in_order(keep, take, near), axis=-1)


VMEM_BYTES = 40 * 1024 * 1024


def dot_rows(left, right):
    return lax.dot_general(left, right, (((1,), (1,)), ((), ())), preferred_element_type=jnp.float32)


def dot_columns(left, right):
    return lax.dot_general(left, right, (((0,), (0,)), ((), ())), preferred_element_type=jnp.float32)


def dot_plain(left, right):
    return jnp.dot(left, right, preferred_element_type=jnp.float32)


def hidden_kernel(
    normed_ref, back_ref, weights_ref, gate_ref, up_ref, hidden_ref, keep_ref, give_ref, held
):
    step = pl.program_id(0)
    rows = weights_ref.shape[3]

    @pl.when(step == 0)
    def _():
        for x in range(NX):
            for z in range(NZ):
                for y in range(NY):
                    start = ((x * NZ + z) * NY + y) * rows
                    for k in range(3):
                        held[k, start : start + rows, :] = weights_ref[x * NY + y, z, k]

    normed = normed_ref[...]
    gate = dot_plain(normed, held[0])
    up = dot_plain(normed, held[1])
    back = dot_plain(back_ref[...], held[2])
    share = jax.nn.sigmoid(gate)
    smooth = gate * share
    hidden_ref[...] = low(smooth * up)
    back_up = low(back * smooth)
    back_gate = low(back * up * (share + smooth * (1.0 - share)))
    gate_ref[...] = back_gate
    up_ref[...] = back_up
    part = dot_rows(back_gate, held[0]) + dot_rows(back_up, held[1])

    @pl.when(step < 2)
    def _():
        give_ref[...] = part

    @pl.when(step >= 2)
    def _():
        keep_ref[...] = part


def hidden_pass(normed, back, weights):
    tokens, width = normed.shape
    units = weights.shape[-1]
    block = tokens // 4
    turned = lambda i: ((i + 2) % 4, 0)
    narrow = jax.ShapeDtypeStruct((tokens, units), jnp.bfloat16)
    half = jax.ShapeDtypeStruct((tokens // 2, width), jnp.float32)
    return pl.pallas_call(
        hidden_kernel,
        grid=(4,),
        in_specs=[
            pl.BlockSpec((block, width), turned),
            pl.BlockSpec((block, width), turned),
            pl.BlockSpec(weights.shape, lambda i: (0, 0, 0, 0, 0)),
        ],
        out_specs=[
            pl.BlockSpec((block, units), turned),
            pl.BlockSpec((block, units), turned),
            pl.BlockSpec((block, units), turned),
            pl.BlockSpec((block, width), lambda i: (jnp.maximum(i - 2, 0), 0)),
            pl.BlockSpec((block, width), lambda i: (jnp.minimum(i, 1), 0)),
        ],
        out_shape=[narrow, narrow, narrow, half, half],
        scratch_shapes=[pltpu.VMEM((3, width, units), jnp.bfloat16)],
        compiler_params=pltpu.CompilerParams(vmem_limit_bytes=VMEM_BYTES),
        cost_estimate=pl.CostEstimate(
            flops=10 * tokens * width * units,
            bytes_accessed=16 * tokens * width,
            transcendentals=tokens * units,
        ),
        name="hidden_pass",
    )(normed, back, weights)


def grads_kernel(
    normed_ref,
    back_ref,
    gate_ref,
    up_ref,
    hidden_ref,
    down_ref,
    grads_ref,
    keep_ref,
    give_ref,
):
    rows, units = down_ref.shape[3:]
    plane = NY * rows
    normed, hidden = normed_ref[...], hidden_ref[...]
    pairs = ((normed, gate_ref[...]), (normed, up_ref[...]), (back_ref[...], hidden))
    for k, (left, right) in enumerate(pairs):
        grad = low(dot_columns(left, right))
        for z in range(NZ):
            part = grad[z * plane : (z + 1) * plane]
            grads_ref[:, z, k] = part.reshape(NY, rows, units)
    down = jnp.concatenate(
        [down_ref[:, z, 0].reshape(plane, units) for z in range(NZ)], axis=0
    )
    half = hidden.shape[0] // 2
    keep_ref[...] = dot_rows(hidden[:half], down)
    give_ref[...] = dot_rows(hidden[half:], down)


def grads_pass(normed, back, gate, up, hidden, weights):
    tokens, width = normed.shape
    rows, units = weights.shape[3:]
    block = width // NX
    column = lambda i: (0, i)
    whole = lambda i: (0, 0)
    half = jax.ShapeDtypeStruct((tokens // 2, width), jnp.float32)
    return pl.pallas_call(
        grads_kernel,
        grid=(NX,),
        in_specs=[
            pl.BlockSpec((tokens, block), column),
            pl.BlockSpec((tokens, block), column),
            pl.BlockSpec((tokens, units), whole),
            pl.BlockSpec((tokens, units), whole),
            pl.BlockSpec((tokens, units), whole),
            pl.BlockSpec((NY, NZ, 1, rows, units), lambda i: (i, 0, 2, 0, 0)),
        ],
        out_specs=[
            pl.BlockSpec((NY, NZ, 3, rows, units), lambda i: (i, 0, 0, 0, 0)),
            pl.BlockSpec((tokens // 2, block), column),
            pl.BlockSpec((tokens // 2, block), column),
        ],
        out_shape=[
            jax.ShapeDtypeStruct(weights.shape, jnp.bfloat16),
            half,
            half,
        ],
        compiler_params=pltpu.CompilerParams(vmem_limit_bytes=VMEM_BYTES),
        cost_estimate=pl.CostEstimate(
            flops=8 * tokens * width * units,
            bytes_accessed=14 * tokens * width,
            transcendentals=0,
        ),
        name="grads_pass",
    )(normed, back, gate, up, hidden, weights)


def mixer_kernel(
    branch_ref,
    weights_ref,
    projected_ref,
    masks_ref,
    taps_ref,
    gated_ref,
    scale_ref,
    branch_part_ref,
    weights_part_ref,
    normed_ref,
    tokens_ref,
    grads_ref,
    back_ref,
    gain_ref,
    conv_ref,
    held,
):
    channels = gated_ref.shape[1]
    rows = grads_ref.shape[2]

    @pl.when(pl.program_id(0) == 0)
    def _():
        count = branch_ref.shape[0]
        back = dot_plain(branch_ref[...], weights_ref[:, 3 * channels : 4 * channels])
        b_part = projected_ref[:, :channels]
        c_part = projected_ref[:, channels : 2 * channels]
        x_part = projected_ref[:, 2 * channels :]
        tap_zero, tap_one, tap_two = taps_ref[0:1], taps_ref[1:2], taps_ref[2:3]
        one, two = masks_ref[:, 0:1] > 0.0, masks_ref[:, 1:2] > 0.0
        product = b_part * x_part
        first = jnp.where(one, pltpu.roll(product, 1, 0), 0.0)
        second = jnp.where(two, pltpu.roll(product, 2, 0), 0.0)
        conv_sum = tap_zero * product + tap_one * first + tap_two * second
        grad = back * c_part
        conv_ref[0:1] = jnp.sum(grad * product, axis=0, keepdims=True)
        conv_ref[1:2] = jnp.sum(grad * first, axis=0, keepdims=True)
        conv_ref[2:3] = jnp.sum(grad * second, axis=0, keepdims=True)
        back_product = tap_zero * grad
        back_product += tap_one * pltpu.roll(jnp.where(one, grad, 0.0), count - 1, 0)
        back_product += tap_two * pltpu.roll(jnp.where(two, grad, 0.0), count - 2, 0)
        held[:, :channels] = low(back_product * x_part)
        held[:, channels : 2 * channels] = low(back * conv_sum)
        held[:, 2 * channels :] = low(back_product * b_part)

    back_projected = held[...]
    plane = NY * rows
    grad_in = low(dot_columns(normed_ref[...], back_projected))
    grad_out = low(dot_columns(branch_part_ref[...], gated_ref[...]))
    for z in range(NZ):
        part = slice(z * plane, (z + 1) * plane)
        grads_ref[:, z, :, : 3 * channels] = grad_in[part].reshape(NY, rows, 3 * channels)
        grads_ref[:, z, :, 3 * channels :] = grad_out[part].reshape(NY, rows, channels)
    back_normed = dot_rows(back_projected, weights_part_ref[:, : 3 * channels])
    back_ref[...] = back_normed
    unit = tokens_ref[...].astype(jnp.float32) * scale_ref[...]
    gain_ref[...] = jnp.sum(back_normed * unit, axis=0, keepdims=True)


def mixer_pass(branch, weights, projected, masks, taps, gated, scale, normed, tokens):
    count, width = branch.shape
    channels = gated.shape[1]
    rows = width // N_DP
    block = width // NX
    whole = lambda i: (0, 0)
    column = pl.BlockSpec((count, block), lambda i: (0, i))
    return pl.pallas_call(
        mixer_kernel,
        grid=(NX,),
        in_specs=[
            pl.BlockSpec(branch.shape, whole),
            pl.BlockSpec(weights.shape, whole),
            pl.BlockSpec(projected.shape, whole),
            pl.BlockSpec(masks.shape, whole),
            pl.BlockSpec(taps.shape, whole),
            pl.BlockSpec(gated.shape, whole),
            pl.BlockSpec(scale.shape, whole),
            column,
            pl.BlockSpec((block, weights.shape[1]), lambda i: (i, 0)),
            column,
            column,
        ],
        out_specs=[
            pl.BlockSpec((NY, NZ, rows, 4 * channels), lambda i: (i, 0, 0, 0)),
            column,
            pl.BlockSpec((1, block), lambda i: (0, i)),
            pl.BlockSpec(taps.shape, whole),
        ],
        out_shape=[
            jax.ShapeDtypeStruct((NX * NY, NZ, rows, 4 * channels), jnp.bfloat16),
            jax.ShapeDtypeStruct((count, width), jnp.float32),
            jax.ShapeDtypeStruct((1, width), jnp.float32),
            jax.ShapeDtypeStruct(taps.shape, jnp.float32),
        ],
        scratch_shapes=[pltpu.VMEM((count, 3 * channels), jnp.bfloat16)],
        compiler_params=pltpu.CompilerParams(vmem_limit_bytes=VMEM_BYTES),
        cost_estimate=pl.CostEstimate(
            flops=16 * count * width * channels,
            bytes_accessed=20 * count * width,
            transcendentals=0,
        ),
        name="mixer_pass",
    )(branch, weights, projected, masks, taps, gated, scale, branch, weights, normed, tokens)


def pieces(value):
    high = lax.reduce_precision(value, 8, 7)
    rest = value - high
    middle = lax.reduce_precision(rest, 8, 7)
    return [low(high), low(middle), low(rest - middle)]


def shards(
    tokens_in,
    cotangent,
    segment_ids,
    in_weight,
    out_weight,
    gate_up_weight,
    down_weight,
    conv_weight,
    norm_gains,
    in_first,
    in_second,
    out_first,
    out_second,
    gate_up_first,
    gate_up_second,
    down_first,
    down_second,
    conv_first,
    conv_second,
    gains_first,
    gains_second,
):
    rows, length, width = tokens_in.shape
    count = rows * length
    taps_n, channels = conv_weight.shape
    units = gate_up_weight.shape[2]
    own_rows = gate_up_weight.shape[1]
    part_units = units // NZ
    core = lax.axis_index("tensor") % 2
    near = (lax.axis_index("dp") // NY) % NZ

    mix_cols = 4 * channels
    low_mix = jnp.concatenate(
        [
            in_weight[0],
            in_weight[1],
            in_weight[2],
            out_weight.T,
            jnp.pad(norm_gains.T, ((0, 0), (0, 126))),
        ],
        axis=1,
    )
    low_mix = low(low_mix)
    low_ffn = low(jnp.concatenate([gate_up_weight, down_weight.T[None]], axis=0))
    keep = lax.dynamic_slice_in_dim(low_ffn, near * part_units, part_units, 2)
    give = lax.dynamic_slice_in_dim(low_ffn, (1 - near) * part_units, part_units, 2)
    take = swap_near(give)
    low_ffn = jnp.stack(in_order(keep, take, near), axis=0)
    ffn_copies = jnp.broadcast_to(low_ffn[None], (NX * NY,) + low_ffn.shape)
    back_out = cotangent.reshape(count, width)
    back_own, back_other = halves(back_out, core)
    back_near = swap_near(back_own)
    back_four = jnp.concatenate([back_own, back_near, back_other, swap_core(back_near)], axis=0)

    flat = wide(tokens_in.reshape(count, width))
    flat_half = halves(flat, core)[0]
    seg_flat = segment_ids.reshape(count)
    place = lax.iota(jnp.int32, count) % length
    mask_one = ((place >= 1) & (seg_flat == jnp.roll(seg_flat, 1)))[:, None]
    mask_two = ((place >= 2) & (seg_flat == jnp.roll(seg_flat, 2)))[:, None]
    masks = wide(jnp.concatenate([mask_one, mask_two], axis=1))
    scale_one = lax.rsqrt(jnp.mean(flat * flat, axis=-1, keepdims=True) + epsilon_norm)

    low_mix = jnp.stack(in_order(low_mix, swap_near(low_mix), near), axis=0)
    mix_full = exchange(jnp.broadcast_to(low_mix[None], (NX * NY,) + low_mix.shape))
    mix_full, ffn_copies, back_four, masks, scale_one = lax.optimization_barrier(
        (mix_full, ffn_copies, back_four, masks, scale_one)
    )
    ffn_full = exchange(ffn_copies)
    mix_full = mix_full.reshape(NX, NY, NZ, own_rows, -1).transpose(0, 2, 1, 3, 4).reshape(width, -1)
    in_full = mix_full[:, : 3 * channels]
    out_full = mix_full[:, 3 * channels : mix_cols]
    gains_value = wide(mix_full[:, mix_cols : mix_cols + 2]).T


    def mixer_local(projected, taps):
        product = projected[:, :channels] * projected[:, 2 * channels :]
        conv_sum = taps[0] * product + taps[1] * jnp.where(
            mask_one, jnp.roll(product, 1, axis=0), 0.0
        )
        conv_sum = conv_sum + taps[2] * jnp.where(mask_two, jnp.roll(product, 2, axis=0), 0.0)
        return projected[:, channels : 2 * channels] * conv_sum

    normed_one = low(rms_gain(flat, gains_value[0]))
    projected = product_of("td,dc->tc", normed_one, in_full)
    gated = low(mixer_local(projected, conv_weight))
    middle = flat_half + sum_four(product_of("tc,dc->td", gated, out_full), core)
    normed_two_f, norm_two_pull = jax.vjp(rms_gain, middle, gains_value[1])
    normed_two = low(normed_two_f)
    normed_two = jnp.concatenate([normed_two, swap_near(normed_two)], axis=0)
    normed_two, ffn_full = lax.optimization_barrier((normed_two, ffn_full))
    normed_two = jnp.concatenate([normed_two, swap_core(normed_two)], axis=0)

    back_gate, back_up, hidden, back_keep, back_give = hidden_pass(
        normed_two, back_four, ffn_full
    )
    back_pair = back_keep + swap_core(back_give)
    back_pair, back_gate, back_up, hidden = lax.optimization_barrier(
        (back_pair, back_gate, back_up, hidden)
    )
    grad_ffn, ffn_keep, ffn_give = grads_pass(
        normed_two, back_four, back_gate, back_up, hidden, ffn_full
    )
    back_normed_two = back_pair[: count // 2] + wide(swap_near(low(back_pair[count // 2 :])))
    back_normed_two, grad_ffn = lax.optimization_barrier((back_normed_two, grad_ffn))
    back_normed_two = across_high(back_normed_two)
    grad_ffn = exchange(grad_ffn)

    ffn_keep, ffn_give, back_normed_two = lax.optimization_barrier(
        (ffn_keep, ffn_give, back_normed_two)
    )
    ffn_pair = ffn_keep + swap_core(ffn_give)
    ffn_half = ffn_pair[: count // 2] + wide(swap_near(low(ffn_pair[count // 2 :])))

    back_middle_norm, grad_gain_two = norm_two_pull(back_normed_two)
    back_middle = wide(back_own) + back_middle_norm
    back_branch = low(back_middle)
    back_branch = joined(back_branch, swap_core(back_branch), core)
    grad_mix, back_normed_one, grad_gain_one, grad_conv = mixer_pass(
        back_branch,
        mix_full,
        projected,
        masks,
        conv_weight,
        gated,
        scale_one,
        normed_one,
        tokens_in.reshape(count, width),
    )
    grad_gains = jnp.concatenate([grad_gain_one, 0.5 * grad_gain_two[None]], axis=0)
    grad_gains = grad_gains.reshape(2, N_DP, own_rows).transpose(1, 0, 2).reshape(N_DP, -1)
    grad_conv = jnp.broadcast_to(grad_conv.reshape(1, -1), (N_DP, grad_conv.size))
    small_size = grad_gains.shape[1] + grad_conv.shape[1]
    small = jnp.concatenate([grad_gains, grad_conv], axis=1)
    small = jnp.pad(small, ((0, 0), (0, 1024 - small_size))).reshape(N_DP, 8, 128)
    small = jnp.concatenate(
        pieces(small) + [jnp.zeros((N_DP, own_rows - 24, 128), jnp.bfloat16)], axis=1
    )
    grad_mix = jnp.concatenate([grad_mix, to_planes(small.reshape(width, 128))], axis=3)
    own, other = halves(back_normed_one, core)
    back_normed_one = own + swap_core(other)
    grad_ffn, grad_mix, back_normed_one = lax.optimization_barrier(
        (grad_ffn, grad_mix, back_normed_one)
    )
    red_mix = jnp.sum(wide(exchange(grad_mix)), axis=0)
    keep = lax.dynamic_index_in_dim(red_mix, near, 0, keepdims=False)
    red_mix = keep + swap_near(lax.dynamic_index_in_dim(red_mix, 1 - near, 0, keepdims=False))
    back_normed_one = across_high(back_normed_one)
    grad_ffn, back_normed_one = lax.optimization_barrier((grad_ffn, back_normed_one))
    red_ffn = whole_units(jnp.sum(wide(grad_ffn), axis=0), near)
    result = middle + across_high(ffn_half)
    result = joined(result, swap_core(result), core)
    back_tokens_norm = jax.vjp(rms_gain, flat_half, gains_value[0])[1](back_normed_one)[0]
    back_tokens = back_middle + back_tokens_norm
    back_tokens = joined(back_tokens, swap_core(back_tokens), core)

    red_small = jnp.sum(red_mix[:24, mix_cols:].reshape(3, 1024), axis=0)
    red_gains = red_small[: norm_gains.size].reshape(norm_gains.shape)
    red_gains = jnp.sum(lax.all_gather(red_gains, "tensor"), axis=0)
    conv_total = red_small[norm_gains.size : small_size].reshape(conv_weight.shape)
    red_in = red_mix[:, : 3 * channels].reshape(-1, 3, channels).transpose(1, 0, 2)
    red_out = red_mix[:, 3 * channels : mix_cols].T
    red_gate_up = red_ffn[:2]
    red_down = red_ffn[2].T
    rate_wide = 0.8 / D**0.5
    rate_down = 0.8 / FF**0.5
    in_new = adam_step(in_weight, red_in, in_first, in_second, rate_wide, 0.1)
    out_new = adam_step(out_weight, red_out, out_first, out_second, rate_wide, 0.1)
    gate_up_new = adam_step(
        gate_up_weight, red_gate_up, gate_up_first, gate_up_second, rate_wide, 0.1
    )
    down_new = adam_step(down_weight, red_down, down_first, down_second, rate_down, 0.1)
    conv_new = adam_step(conv_weight, conv_total, conv_first, conv_second, 1.0, 0.0)
    gains_new = adam_step(norm_gains, red_gains, gains_first, gains_second, 0.3, 0.0)
    return (
        result.reshape(rows, length, width),
        back_tokens.reshape(rows, length, width),
        in_new[0],
        in_new[1],
        in_new[2],
        out_new[0],
        out_new[1],
        out_new[2],
        gate_up_new[0],
        gate_up_new[1],
        gate_up_new[2],
        down_new[0],
        down_new[1],
        down_new[2],
        conv_new[0],
        conv_new[1],
        conv_new[2],
        gains_new[0],
        gains_new[1],
        gains_new[2],
    )


def solution(mesh):
    in_specs = (
        P("dp", None, None),
        P("dp", None, None),
        P("dp", None),
        P(None, "dp", "tensor"),
        P("tensor", "dp"),
        P(None, "dp", "tensor"),
        P("tensor", "dp"),
        P(None, "tensor"),
        P(None, "dp"),
        P(None, "dp", "tensor"),
        P(None, "dp", "tensor"),
        P("tensor", "dp"),
        P("tensor", "dp"),
        P(None, "dp", "tensor"),
        P(None, "dp", "tensor"),
        P("tensor", "dp"),
        P("tensor", "dp"),
        P(None, "tensor"),
        P(None, "tensor"),
        P(None, "dp"),
        P(None, "dp"),
    )
    out_specs = (
        P("dp", None, None),
        P("dp", None, None),
        P(None, "dp", "tensor"),
        P(None, "dp", "tensor"),
        P(None, "dp", "tensor"),
        P("tensor", "dp"),
        P("tensor", "dp"),
        P("tensor", "dp"),
        P(None, "dp", "tensor"),
        P(None, "dp", "tensor"),
        P(None, "dp", "tensor"),
        P("tensor", "dp"),
        P("tensor", "dp"),
        P("tensor", "dp"),
        P(None, "tensor"),
        P(None, "tensor"),
        P(None, "tensor"),
        P(None, "dp"),
        P(None, "dp"),
        P(None, "dp"),
    )
    return jax.shard_map(shards, mesh=mesh, in_specs=in_specs, out_specs=out_specs, check_vma=False)
```

```python
import jax
import jax.numpy as jnp
from jax import lax
from jax.experimental import pallas as pl
from jax.experimental.pallas import tpu as pltpu
from jax.sharding import PartitionSpec as P

D = 1024
FF = 4608
ADAM_STEP = 10
NX, NZ, NY = 4, 2, 4
N_DP = NX * NZ * NY
NEAR_PAIRS = [(d, d ^ NY) for d in range(N_DP)]
PLANES = [[(x * NZ + z) * NY + y for x in range(NX) for y in range(NY)] for z in range(NZ)]
CORE_PAIRS = [(0, 1), (1, 0), (2, 3), (3, 2)]
HIGH_PAIRS = [(0, 2), (2, 0), (1, 3), (3, 1)]


epsilon_norm = 1e-05
epsilon_adam = 1e-08
beta_one = 0.9
beta_two = 0.95


def rms_gain(values, gain_row):
    return (
        values
        * lax.rsqrt(jnp.mean(values * values, axis=-1, keepdims=True) + epsilon_norm)
        * gain_row
    )


def adam_step(master, gradient, first, second, step_rate, decay_rate):
    first_new = beta_one * first + (1.0 - beta_one) * gradient
    second_new = beta_two * second + (1.0 - beta_two) * gradient * gradient
    first_hat = first_new / (1.0 - beta_one**ADAM_STEP)
    second_hat = second_new / (1.0 - beta_two**ADAM_STEP)
    master_new = master - step_rate * (
        first_hat / (jnp.sqrt(second_hat) + epsilon_adam) + decay_rate * master
    )
    return (master_new, first_new, second_new)


def swap_core(value):
    return lax.ppermute(value, "tensor", CORE_PAIRS)


def swap_high(value):
    return lax.ppermute(value, "tensor", HIGH_PAIRS)


def swap_near(value):
    return lax.ppermute(value, "dp", NEAR_PAIRS)


def low(value):
    return value.astype(jnp.bfloat16)


def wide(value):
    return value.astype(jnp.float32)


def product_of(spec, left, right):
    return jnp.einsum(spec, left, right, preferred_element_type=jnp.float32)


def halves(value, core):
    half = value.shape[0] // 2
    return (
        lax.dynamic_slice_in_dim(value, core * half, half, 0),
        lax.dynamic_slice_in_dim(value, (1 - core) * half, half, 0),
    )


def joined(own, other, core):
    first = core == 0
    return jnp.concatenate([jnp.where(first, own, other), jnp.where(first, other, own)], axis=0)


def across_high(value):
    value = low(value)
    return wide(value) + wide(swap_high(value))


def sum_four(part, core):
    own, other = halves(part, core)
    return across_high(own + swap_core(other))


def to_planes(grad):
    columns = grad.shape[1]
    blocks = grad.reshape(NX, NZ, NY, -1, columns).transpose(0, 2, 1, 3, 4)
    return blocks.reshape(NX * NY, NZ, -1, columns)


def exchange(blocks):
    return lax.all_to_all(blocks, "dp", 0, 0, tiled=True, axis_index_groups=PLANES)


def in_order(mine, theirs, near):
    first = near == 0
    return jnp.where(first, mine, theirs), jnp.where(first, theirs, mine)


def whole_units(grad, near):
    keep = lax.dynamic_index_in_dim(grad, near, 0, keepdims=False)
    take = swap_near(lax.dynamic_index_in_dim(grad, 1 - near, 0, keepdims=False))
    return jnp.concatenate(in_order(keep, take, near), axis=-1)


def spread_kernel(block_ref, copies_ref):
    copies_ref[0] = block_ref[...]


def spread_pass(block):
    return pl.pallas_call(
        spread_kernel,
        grid=(NX * NY,),
        in_specs=[pl.BlockSpec(block.shape, lambda i: (0,) * block.ndim)],
        out_specs=pl.BlockSpec((1,) + block.shape, lambda i: (i,) + (0,) * block.ndim),
        out_shape=jax.ShapeDtypeStruct((NX * NY,) + block.shape, block.dtype),
        compiler_params=pltpu.CompilerParams(vmem_limit_bytes=VMEM_BYTES),
        cost_estimate=pl.CostEstimate(
            flops=0, bytes_accessed=2 * NX * NY * block.size, transcendentals=0
        ),
        name="spread_pass",
    )(block)


VMEM_BYTES = 40 * 1024 * 1024


def dot_rows(left, right):
    return lax.dot_general(left, right, (((1,), (1,)), ((), ())), preferred_element_type=jnp.float32)


def dot_columns(left, right):
    return lax.dot_general(left, right, (((0,), (0,)), ((), ())), preferred_element_type=jnp.float32)


def dot_plain(left, right):
    return jnp.dot(left, right, preferred_element_type=jnp.float32)


def hidden_kernel(
    normed_ref, back_ref, weights_ref, gate_ref, up_ref, hidden_ref, keep_ref, give_ref, held
):
    step = pl.program_id(0)
    rows = weights_ref.shape[3]

    @pl.when(step == 0)
    def _():
        for x in range(NX):
            for z in range(NZ):
                for y in range(NY):
                    start = ((x * NZ + z) * NY + y) * rows
                    for k in range(3):
                        held[k, start : start + rows, :] = weights_ref[x * NY + y, z, k]

    normed = normed_ref[...]
    gate = dot_plain(normed, held[0])
    up = dot_plain(normed, held[1])
    back = dot_plain(back_ref[...], held[2])
    share = jax.nn.sigmoid(gate)
    smooth = gate * share
    hidden_ref[...] = low(smooth * up)
    back_up = low(back * smooth)
    back_gate = low(back * up * (share + smooth * (1.0 - share)))
    gate_ref[...] = back_gate
    up_ref[...] = back_up
    part = dot_rows(back_gate, held[0]) + dot_rows(back_up, held[1])

    @pl.when(step < 2)
    def _():
        give_ref[...] = part

    @pl.when(step >= 2)
    def _():
        keep_ref[...] = part


def hidden_pass(normed, back, weights):
    tokens, width = normed.shape
    units = weights.shape[-1]
    block = tokens // 4
    turned = lambda i: ((i + 2) % 4, 0)
    narrow = jax.ShapeDtypeStruct((tokens, units), jnp.bfloat16)
    half = jax.ShapeDtypeStruct((tokens // 2, width), jnp.float32)
    return pl.pallas_call(
        hidden_kernel,
        grid=(4,),
        in_specs=[
            pl.BlockSpec((block, width), turned),
            pl.BlockSpec((block, width), turned),
            pl.BlockSpec(weights.shape, lambda i: (0, 0, 0, 0, 0)),
        ],
        out_specs=[
            pl.BlockSpec((block, units), turned),
            pl.BlockSpec((block, units), turned),
            pl.BlockSpec((block, units), turned),
            pl.BlockSpec((block, width), lambda i: (jnp.maximum(i - 2, 0), 0)),
            pl.BlockSpec((block, width), lambda i: (jnp.minimum(i, 1), 0)),
        ],
        out_shape=[narrow, narrow, narrow, half, half],
        scratch_shapes=[pltpu.VMEM((3, width, units), jnp.bfloat16)],
        compiler_params=pltpu.CompilerParams(vmem_limit_bytes=VMEM_BYTES),
        cost_estimate=pl.CostEstimate(
            flops=10 * tokens * width * units,
            bytes_accessed=16 * tokens * width,
            transcendentals=tokens * units,
        ),
        name="hidden_pass",
    )(normed, back, weights)


def grads_kernel(
    normed_ref,
    back_ref,
    gate_ref,
    up_ref,
    hidden_ref,
    down_ref,
    grads_ref,
    keep_ref,
    give_ref,
):
    rows, units = down_ref.shape[3:]
    plane = NY * rows
    normed, hidden = normed_ref[...], hidden_ref[...]
    pairs = ((normed, gate_ref[...]), (normed, up_ref[...]), (back_ref[...], hidden))
    for k, (left, right) in enumerate(pairs):
        grad = low(dot_columns(left, right))
        for z in range(NZ):
            part = grad[z * plane : (z + 1) * plane]
            grads_ref[:, z, k] = part.reshape(NY, rows, units)
    down = jnp.concatenate(
        [down_ref[:, z, 0].reshape(plane, units) for z in range(NZ)], axis=0
    )
    half = hidden.shape[0] // 2
    keep_ref[...] = dot_rows(hidden[:half], down)
    give_ref[...] = dot_rows(hidden[half:], down)


def grads_pass(normed, back, gate, up, hidden, weights):
    tokens, width = normed.shape
    rows, units = weights.shape[3:]
    block = width // NX
    column = lambda i: (0, i)
    whole = lambda i: (0, 0)
    half = jax.ShapeDtypeStruct((tokens // 2, width), jnp.float32)
    return pl.pallas_call(
        grads_kernel,
        grid=(NX,),
        in_specs=[
            pl.BlockSpec((tokens, block), column),
            pl.BlockSpec((tokens, block), column),
            pl.BlockSpec((tokens, units), whole),
            pl.BlockSpec((tokens, units), whole),
            pl.BlockSpec((tokens, units), whole),
            pl.BlockSpec((NY, NZ, 1, rows, units), lambda i: (i, 0, 2, 0, 0)),
        ],
        out_specs=[
            pl.BlockSpec((NY, NZ, 3, rows, units), lambda i: (i, 0, 0, 0, 0)),
            pl.BlockSpec((tokens // 2, block), column),
            pl.BlockSpec((tokens // 2, block), column),
        ],
        out_shape=[
            jax.ShapeDtypeStruct(weights.shape, jnp.bfloat16),
            half,
            half,
        ],
        compiler_params=pltpu.CompilerParams(vmem_limit_bytes=VMEM_BYTES),
        cost_estimate=pl.CostEstimate(
            flops=8 * tokens * width * units,
            bytes_accessed=14 * tokens * width,
            transcendentals=0,
        ),
        name="grads_pass",
    )(normed, back, gate, up, hidden, weights)


def mixer_kernel(
    branch_ref,
    weights_ref,
    projected_ref,
    masks_ref,
    taps_ref,
    gated_ref,
    scale_ref,
    branch_part_ref,
    weights_part_ref,
    normed_ref,
    tokens_ref,
    grads_ref,
    back_ref,
    gain_ref,
    conv_ref,
    held,
):
    channels = gated_ref.shape[1]
    rows = grads_ref.shape[2]

    @pl.when(pl.program_id(0) == 0)
    def _():
        count = branch_ref.shape[0]
        back = dot_plain(branch_ref[...], weights_ref[:, 3 * channels : 4 * channels])
        b_part = projected_ref[:, :channels]
        c_part = projected_ref[:, channels : 2 * channels]
        x_part = projected_ref[:, 2 * channels :]
        tap_zero, tap_one, tap_two = taps_ref[0:1], taps_ref[1:2], taps_ref[2:3]
        one, two = masks_ref[:, 0:1] > 0.0, masks_ref[:, 1:2] > 0.0
        product = b_part * x_part
        first = jnp.where(one, pltpu.roll(product, 1, 0), 0.0)
        second = jnp.where(two, pltpu.roll(product, 2, 0), 0.0)
        conv_sum = tap_zero * product + tap_one * first + tap_two * second
        grad = back * c_part
        conv_ref[0:1] = jnp.sum(grad * product, axis=0, keepdims=True)
        conv_ref[1:2] = jnp.sum(grad * first, axis=0, keepdims=True)
        conv_ref[2:3] = jnp.sum(grad * second, axis=0, keepdims=True)
        back_product = tap_zero * grad
        back_product += tap_one * pltpu.roll(jnp.where(one, grad, 0.0), count - 1, 0)
        back_product += tap_two * pltpu.roll(jnp.where(two, grad, 0.0), count - 2, 0)
        held[:, :channels] = low(back_product * x_part)
        held[:, channels : 2 * channels] = low(back * conv_sum)
        held[:, 2 * channels :] = low(back_product * b_part)

    back_projected = held[...]
    plane = NY * rows
    grad_in = low(dot_columns(normed_ref[...], back_projected))
    grad_out = low(dot_columns(branch_part_ref[...], gated_ref[...]))
    for z in range(NZ):
        part = slice(z * plane, (z + 1) * plane)
        grads_ref[:, z, :, : 3 * channels] = grad_in[part].reshape(NY, rows, 3 * channels)
        grads_ref[:, z, :, 3 * channels :] = grad_out[part].reshape(NY, rows, channels)
    back_normed = dot_rows(back_projected, weights_part_ref[:, : 3 * channels])
    back_ref[...] = back_normed
    unit = tokens_ref[...].astype(jnp.float32) * scale_ref[...]
    gain_ref[...] = jnp.sum(back_normed * unit, axis=0, keepdims=True)


def mixer_pass(branch, weights, projected, masks, taps, gated, scale, normed, tokens):
    count, width = branch.shape
    channels = gated.shape[1]
    rows = width // N_DP
    block = width // NX
    whole = lambda i: (0, 0)
    column = pl.BlockSpec((count, block), lambda i: (0, i))
    return pl.pallas_call(
        mixer_kernel,
        grid=(NX,),
        in_specs=[
            pl.BlockSpec(branch.shape, whole),
            pl.BlockSpec(weights.shape, whole),
            pl.BlockSpec(projected.shape, whole),
            pl.BlockSpec(masks.shape, whole),
            pl.BlockSpec(taps.shape, whole),
            pl.BlockSpec(gated.shape, whole),
            pl.BlockSpec(scale.shape, whole),
            column,
            pl.BlockSpec((block, weights.shape[1]), lambda i: (i, 0)),
            column,
            column,
        ],
        out_specs=[
            pl.BlockSpec((NY, NZ, rows, 4 * channels), lambda i: (i, 0, 0, 0)),
            column,
            pl.BlockSpec((1, block), lambda i: (0, i)),
            pl.BlockSpec(taps.shape, whole),
        ],
        out_shape=[
            jax.ShapeDtypeStruct((NX * NY, NZ, rows, 4 * channels), jnp.bfloat16),
            jax.ShapeDtypeStruct((count, width), jnp.float32),
            jax.ShapeDtypeStruct((1, width), jnp.float32),
            jax.ShapeDtypeStruct(taps.shape, jnp.float32),
        ],
        scratch_shapes=[pltpu.VMEM((count, 3 * channels), jnp.bfloat16)],
        compiler_params=pltpu.CompilerParams(vmem_limit_bytes=VMEM_BYTES),
        cost_estimate=pl.CostEstimate(
            flops=16 * count * width * channels,
            bytes_accessed=20 * count * width,
            transcendentals=0,
        ),
        name="mixer_pass",
    )(branch, weights, projected, masks, taps, gated, scale, branch, weights, normed, tokens)


def pieces(value):
    high = lax.reduce_precision(value, 8, 7)
    rest = value - high
    middle = lax.reduce_precision(rest, 8, 7)
    return [low(high), low(middle), low(rest - middle)]


def shards(
    tokens_in,
    cotangent,
    segment_ids,
    in_weight,
    out_weight,
    gate_up_weight,
    down_weight,
    conv_weight,
    norm_gains,
    in_first,
    in_second,
    out_first,
    out_second,
    gate_up_first,
    gate_up_second,
    down_first,
    down_second,
    conv_first,
    conv_second,
    gains_first,
    gains_second,
):
    rows, length, width = tokens_in.shape
    count = rows * length
    taps_n, channels = conv_weight.shape
    units = gate_up_weight.shape[2]
    own_rows = gate_up_weight.shape[1]
    part_units = units // NZ
    core = lax.axis_index("tensor") % 2
    near = (lax.axis_index("dp") // NY) % NZ

    mix_cols = 4 * channels
    low_mix = jnp.concatenate(
        [
            in_weight[0],
            in_weight[1],
            in_weight[2],
            out_weight.T,
            jnp.pad(norm_gains.T, ((0, 0), (0, 126))),
        ],
        axis=1,
    )
    low_mix = low(low_mix)
    low_mix = jnp.stack(in_order(low_mix, swap_near(low_mix), near), axis=0)
    low_mix, gate_up_early, down_early, cotangent, tokens_in, segment_ids = (
        lax.optimization_barrier(
            (low_mix, gate_up_weight, down_weight, cotangent, tokens_in, segment_ids)
        )
    )
    low_ffn = low(jnp.concatenate([gate_up_early, down_early.T[None]], axis=0))
    keep = lax.dynamic_slice_in_dim(low_ffn, near * part_units, part_units, 2)
    give = lax.dynamic_slice_in_dim(low_ffn, (1 - near) * part_units, part_units, 2)
    take = swap_near(give)
    low_ffn = jnp.stack(in_order(keep, take, near), axis=0)
    ffn_copies = spread_pass(low_ffn)
    back_out = cotangent.reshape(count, width)
    back_own, back_other = halves(back_out, core)
    back_near = swap_near(back_own)
    back_four = jnp.concatenate([back_own, back_near, back_other, swap_core(back_near)], axis=0)

    flat = wide(tokens_in.reshape(count, width))
    flat_half = halves(flat, core)[0]
    seg_flat = segment_ids.reshape(count)
    place = lax.iota(jnp.int32, count) % length
    mask_one = ((place >= 1) & (seg_flat == jnp.roll(seg_flat, 1)))[:, None]
    mask_two = ((place >= 2) & (seg_flat == jnp.roll(seg_flat, 2)))[:, None]
    masks = wide(jnp.concatenate([mask_one, mask_two], axis=1))
    scale_one = lax.rsqrt(jnp.mean(flat * flat, axis=-1, keepdims=True) + epsilon_norm)

    mix_full = exchange(jnp.broadcast_to(low_mix[None], (NX * NY,) + low_mix.shape))
    mix_full, ffn_copies, back_four, masks, scale_one = lax.optimization_barrier(
        (mix_full, ffn_copies, back_four, masks, scale_one)
    )
    ffn_full = exchange(ffn_copies)
    mix_full = mix_full.reshape(NX, NY, NZ, own_rows, -1).transpose(0, 2, 1, 3, 4).reshape(width, -1)
    in_full = mix_full[:, : 3 * channels]
    out_full = mix_full[:, 3 * channels : mix_cols]
    gains_value = wide(mix_full[:, mix_cols : mix_cols + 2]).T


    def mixer_local(projected, taps):
        product = projected[:, :channels] * projected[:, 2 * channels :]
        conv_sum = taps[0] * product + taps[1] * jnp.where(
            mask_one, jnp.roll(product, 1, axis=0), 0.0
        )
        conv_sum = conv_sum + taps[2] * jnp.where(mask_two, jnp.roll(product, 2, axis=0), 0.0)
        return projected[:, channels : 2 * channels] * conv_sum

    normed_one = low(rms_gain(flat, gains_value[0]))
    projected = product_of("td,dc->tc", normed_one, in_full)
    gated = low(mixer_local(projected, conv_weight))
    middle = flat_half + sum_four(product_of("tc,dc->td", gated, out_full), core)
    normed_two_f, norm_two_pull = jax.vjp(rms_gain, middle, gains_value[1])
    normed_two = low(normed_two_f)
    normed_two = jnp.concatenate([normed_two, swap_near(normed_two)], axis=0)
    normed_two, ffn_full = lax.optimization_barrier((normed_two, ffn_full))
    normed_two = jnp.concatenate([normed_two, swap_core(normed_two)], axis=0)

    back_gate, back_up, hidden, back_keep, back_give = hidden_pass(
        normed_two, back_four, ffn_full
    )
    back_pair = back_keep + swap_core(back_give)
    back_pair, back_gate, back_up, hidden = lax.optimization_barrier(
        (back_pair, back_gate, back_up, hidden)
    )
    grad_ffn, ffn_keep, ffn_give = grads_pass(
        normed_two, back_four, back_gate, back_up, hidden, ffn_full
    )
    back_normed_two = back_pair[: count // 2] + wide(swap_near(low(back_pair[count // 2 :])))
    back_normed_two, grad_ffn = lax.optimization_barrier((back_normed_two, grad_ffn))
    back_normed_two = across_high(back_normed_two)
    grad_ffn = exchange(grad_ffn)

    ffn_keep, ffn_give, back_normed_two = lax.optimization_barrier(
        (ffn_keep, ffn_give, back_normed_two)
    )
    ffn_pair = ffn_keep + swap_core(ffn_give)
    ffn_half = ffn_pair[: count // 2] + wide(swap_near(low(ffn_pair[count // 2 :])))

    back_middle_norm, grad_gain_two = norm_two_pull(back_normed_two)
    back_middle = wide(back_own) + back_middle_norm
    back_branch = low(back_middle)
    back_branch = joined(back_branch, swap_core(back_branch), core)
    grad_mix, back_normed_one, grad_gain_one, grad_conv = mixer_pass(
        back_branch,
        mix_full,
        projected,
        masks,
        conv_weight,
        gated,
        scale_one,
        normed_one,
        tokens_in.reshape(count, width),
    )
    grad_gains = jnp.concatenate([grad_gain_one, 0.5 * grad_gain_two[None]], axis=0)
    grad_gains = grad_gains.reshape(2, N_DP, own_rows).transpose(1, 0, 2).reshape(N_DP, -1)
    grad_conv = jnp.broadcast_to(grad_conv.reshape(1, -1), (N_DP, grad_conv.size))
    small_size = grad_gains.shape[1] + grad_conv.shape[1]
    small = jnp.concatenate([grad_gains, grad_conv], axis=1)
    small = jnp.pad(small, ((0, 0), (0, 1024 - small_size))).reshape(N_DP, 8, 128)
    small = jnp.concatenate(
        pieces(small) + [jnp.zeros((N_DP, own_rows - 24, 128), jnp.bfloat16)], axis=1
    )
    grad_mix = jnp.concatenate([grad_mix, to_planes(small.reshape(width, 128))], axis=3)
    own, other = halves(back_normed_one, core)
    back_normed_one = own + swap_core(other)
    grad_ffn, grad_mix, back_normed_one = lax.optimization_barrier(
        (grad_ffn, grad_mix, back_normed_one)
    )
    red_mix = jnp.sum(wide(exchange(grad_mix)), axis=0)
    keep = lax.dynamic_index_in_dim(red_mix, near, 0, keepdims=False)
    red_mix = keep + swap_near(lax.dynamic_index_in_dim(red_mix, 1 - near, 0, keepdims=False))
    back_normed_one = across_high(back_normed_one)
    grad_ffn, back_normed_one, ffn_half = lax.optimization_barrier(
        (grad_ffn, back_normed_one, ffn_half)
    )
    red_ffn = whole_units(jnp.sum(wide(grad_ffn), axis=0), near)
    result = middle + across_high(ffn_half)
    result = joined(result, swap_core(result), core)
    back_tokens_norm = jax.vjp(rms_gain, flat_half, gains_value[0])[1](back_normed_one)[0]
    back_tokens = back_middle + back_tokens_norm
    back_tokens = joined(back_tokens, swap_core(back_tokens), core)

    red_small = jnp.sum(red_mix[:24, mix_cols:].reshape(3, 1024), axis=0)
    red_gains = red_small[: norm_gains.size].reshape(norm_gains.shape)
    red_gains = jnp.sum(lax.all_gather(red_gains, "tensor"), axis=0)
    conv_total = red_small[norm_gains.size : small_size].reshape(conv_weight.shape)
    red_in = red_mix[:, : 3 * channels].reshape(-1, 3, channels).transpose(1, 0, 2)
    red_out = red_mix[:, 3 * channels : mix_cols].T
    red_gate_up = red_ffn[:2]
    red_down = red_ffn[2].T
    rate_wide = 0.8 / D**0.5
    rate_down = 0.8 / FF**0.5
    in_new = adam_step(in_weight, red_in, in_first, in_second, rate_wide, 0.1)
    out_new = adam_step(out_weight, red_out, out_first, out_second, rate_wide, 0.1)
    gate_up_new = adam_step(
        gate_up_weight, red_gate_up, gate_up_first, gate_up_second, rate_wide, 0.1
    )
    down_new = adam_step(down_weight, red_down, down_first, down_second, rate_down, 0.1)
    conv_new = adam_step(conv_weight, conv_total, conv_first, conv_second, 1.0, 0.0)
    gains_new = adam_step(norm_gains, red_gains, gains_first, gains_second, 0.3, 0.0)
    return (
        result.reshape(rows, length, width),
        back_tokens.reshape(rows, length, width),
        in_new[0],
        in_new[1],
        in_new[2],
        out_new[0],
        out_new[1],
        out_new[2],
        gate_up_new[0],
        gate_up_new[1],
        gate_up_new[2],
        down_new[0],
        down_new[1],
        down_new[2],
        conv_new[0],
        conv_new[1],
        conv_new[2],
        gains_new[0],
        gains_new[1],
        gains_new[2],
    )


def solution(mesh):
    in_specs = (
        P("dp", None, None),
        P("dp", None, None),
        P("dp", None),
        P(None, "dp", "tensor"),
        P("tensor", "dp"),
        P(None, "dp", "tensor"),
        P("tensor", "dp"),
        P(None, "tensor"),
        P(None, "dp"),
        P(None, "dp", "tensor"),
        P(None, "dp", "tensor"),
        P("tensor", "dp"),
        P("tensor", "dp"),
        P(None, "dp", "tensor"),
        P(None, "dp", "tensor"),
        P("tensor", "dp"),
        P("tensor", "dp"),
        P(None, "tensor"),
        P(None, "tensor"),
        P(None, "dp"),
        P(None, "dp"),
    )
    out_specs = (
        P("dp", None, None),
        P("dp", None, None),
        P(None, "dp", "tensor"),
        P(None, "dp", "tensor"),
        P(None, "dp", "tensor"),
        P("tensor", "dp"),
        P("tensor", "dp"),
        P("tensor", "dp"),
        P(None, "dp", "tensor"),
        P(None, "dp", "tensor"),
        P(None, "dp", "tensor"),
        P("tensor", "dp"),
        P("tensor", "dp"),
        P("tensor", "dp"),
        P(None, "tensor"),
        P(None, "tensor"),
        P(None, "tensor"),
        P(None, "dp"),
        P(None, "dp"),
        P(None, "dp"),
    )
    return jax.shard_map(shards, mesh=mesh, in_specs=in_specs, out_specs=out_specs, check_vma=False)
```

```python
import jax
import jax.numpy as jnp
from jax import lax
from jax.experimental import pallas as pl
from jax.experimental.pallas import tpu as pltpu
from jax.sharding import PartitionSpec as P

D = 1024
FF = 4608
ADAM_STEP = 10
NX, NZ, NY = 4, 2, 4
N_DP = NX * NZ * NY
NEAR_PAIRS = [(d, d ^ NY) for d in range(N_DP)]
PLANES = [[(x * NZ + z) * NY + y for x in range(NX) for y in range(NY)] for z in range(NZ)]
CORE_PAIRS = [(0, 1), (1, 0), (2, 3), (3, 2)]
HIGH_PAIRS = [(0, 2), (2, 0), (1, 3), (3, 1)]


epsilon_norm = 1e-05
epsilon_adam = 1e-08
beta_one = 0.9
beta_two = 0.95


def rms_gain(values, gain_row):
    return (
        values
        * lax.rsqrt(jnp.mean(values * values, axis=-1, keepdims=True) + epsilon_norm)
        * gain_row
    )


def adam_step(master, gradient, first, second, step_rate, decay_rate):
    first_new = beta_one * first + (1.0 - beta_one) * gradient
    second_new = beta_two * second + (1.0 - beta_two) * gradient * gradient
    first_hat = first_new / (1.0 - beta_one**ADAM_STEP)
    second_hat = second_new / (1.0 - beta_two**ADAM_STEP)
    master_new = master - step_rate * (
        first_hat / (jnp.sqrt(second_hat) + epsilon_adam) + decay_rate * master
    )
    return (master_new, first_new, second_new)


def swap_core(value):
    return lax.ppermute(value, "tensor", CORE_PAIRS)


def swap_high(value):
    return lax.ppermute(value, "tensor", HIGH_PAIRS)


def swap_near(value):
    return lax.ppermute(value, "dp", NEAR_PAIRS)


def low(value):
    return value.astype(jnp.bfloat16)


def wide(value):
    return value.astype(jnp.float32)


def product_of(spec, left, right):
    return jnp.einsum(spec, left, right, preferred_element_type=jnp.float32)


def halves(value, core):
    half = value.shape[0] // 2
    return (
        lax.dynamic_slice_in_dim(value, core * half, half, 0),
        lax.dynamic_slice_in_dim(value, (1 - core) * half, half, 0),
    )


def joined(own, other, core):
    first = core == 0
    return jnp.concatenate([jnp.where(first, own, other), jnp.where(first, other, own)], axis=0)


def across_high(value):
    value = low(value)
    return wide(value) + wide(swap_high(value))


def sum_four(part, core):
    own, other = halves(part, core)
    return across_high(own + swap_core(other))


def to_planes(grad):
    columns = grad.shape[1]
    blocks = grad.reshape(NX, NZ, NY, -1, columns).transpose(0, 2, 1, 3, 4)
    return blocks.reshape(NX * NY, NZ, -1, columns)


def exchange(blocks):
    return lax.all_to_all(blocks, "dp", 0, 0, tiled=True, axis_index_groups=PLANES)


def in_order(mine, theirs, near):
    first = near == 0
    return jnp.where(first, mine, theirs), jnp.where(first, theirs, mine)


def places(units):
    main = units // 128 * 128
    rest = units - main
    return main, [(k * main, 3 * main + k * rest, 3 * main + (k + 1) * rest) for k in range(3)]


def packed(three):
    main = places(three.shape[2])[0]
    parts = [three[k, :, :main] for k in range(3)] + [three[k, :, main:] for k in range(3)]
    return jnp.concatenate(parts, axis=1)


def unpacked(rows):
    main, where = places(rows.shape[1] // 3)
    return jnp.stack(
        [
            jnp.concatenate([rows[:, start : start + main], rows[:, tail:end]], axis=1)
            for start, tail, end in where
        ]
    )


def whole_units(grad, near):
    keep = lax.dynamic_index_in_dim(grad, near, 0, keepdims=False)
    take = swap_near(lax.dynamic_index_in_dim(grad, 1 - near, 0, keepdims=False))
    return jnp.concatenate(in_order(unpacked(keep), unpacked(take), near), axis=2)


VMEM_BYTES = 40 * 1024 * 1024


def dot_rows(left, right):
    return lax.dot_general(left, right, (((1,), (1,)), ((), ())), preferred_element_type=jnp.float32)


def dot_columns(left, right):
    return lax.dot_general(left, right, (((0,), (0,)), ((), ())), preferred_element_type=jnp.float32)


def dot_plain(left, right):
    return jnp.dot(left, right, preferred_element_type=jnp.float32)


def hidden_kernel(
    normed_ref, back_ref, weights_ref, gate_ref, up_ref, hidden_ref, keep_ref, give_ref, held
):
    step = pl.program_id(0)
    rows = weights_ref.shape[2]
    main, where = places(gate_ref.shape[1])

    @pl.when(step == 0)
    def _():
        for x in range(NX):
            for z in range(NZ):
                for y in range(NY):
                    start = ((x * NZ + z) * NY + y) * rows
                    for k, (first, tail, end) in enumerate(where):
                        block = weights_ref.at[x * NY + y, z]
                        held[k, start : start + rows, :main] = block[:, first : first + main]
                        held[k, start : start + rows, main:] = block[:, tail:end]

    normed = normed_ref[...]
    gate = dot_plain(normed, held[0])
    up = dot_plain(normed, held[1])
    back = dot_plain(back_ref[...], held[2])
    share = jax.nn.sigmoid(gate)
    smooth = gate * share
    hidden_ref[...] = low(smooth * up)
    back_up = low(back * smooth)
    back_gate = low(back * up * (share + smooth * (1.0 - share)))
    gate_ref[...] = back_gate
    up_ref[...] = back_up
    part = dot_rows(back_gate, held[0]) + dot_rows(back_up, held[1])

    @pl.when(step < 2)
    def _():
        give_ref[...] = part

    @pl.when(step >= 2)
    def _():
        keep_ref[...] = part


def hidden_pass(normed, back, weights):
    tokens, width = normed.shape
    units = weights.shape[-1] // 3
    block = tokens // 4
    turned = lambda i: ((i + 2) % 4, 0)
    narrow = jax.ShapeDtypeStruct((tokens, units), jnp.bfloat16)
    half = jax.ShapeDtypeStruct((tokens // 2, width), jnp.float32)
    return pl.pallas_call(
        hidden_kernel,
        grid=(4,),
        in_specs=[
            pl.BlockSpec((block, width), turned),
            pl.BlockSpec((block, width), turned),
            pl.BlockSpec(weights.shape, lambda i: (0, 0, 0, 0)),
        ],
        out_specs=[
            pl.BlockSpec((block, units), turned),
            pl.BlockSpec((block, units), turned),
            pl.BlockSpec((block, units), turned),
            pl.BlockSpec((block, width), lambda i: (jnp.maximum(i - 2, 0), 0)),
            pl.BlockSpec((block, width), lambda i: (jnp.minimum(i, 1), 0)),
        ],
        out_shape=[narrow, narrow, narrow, half, half],
        scratch_shapes=[pltpu.VMEM((3, width, units), jnp.bfloat16)],
        compiler_params=pltpu.CompilerParams(vmem_limit_bytes=VMEM_BYTES),
        cost_estimate=pl.CostEstimate(
            flops=10 * tokens * width * units,
            bytes_accessed=16 * tokens * width,
            transcendentals=tokens * units,
        ),
        name="hidden_pass",
    )(normed, back, weights)


def grads_kernel(
    normed_ref,
    back_ref,
    gate_ref,
    up_ref,
    hidden_ref,
    weights_ref,
    grads_ref,
    keep_ref,
    give_ref,
    down,
):
    rows = weights_ref.shape[2]
    units = hidden_ref.shape[1]
    plane = NY * rows
    main, where = places(units)
    normed, hidden = normed_ref[...], hidden_ref[...]
    pairs = ((normed, gate_ref[...]), (normed, up_ref[...]), (back_ref[...], hidden))
    for (left, right), (first, tail, end) in zip(pairs, where):
        grad = low(dot_columns(left, right))
        for z in range(NZ):
            part = grad[z * plane : (z + 1) * plane]
            grads_ref[:, z, :, first : first + main] = part[:, :main].reshape(NY, rows, main)
            grads_ref[:, z, :, tail:end] = part[:, main:].reshape(NY, rows, end - tail)
    first, tail, end = where[2]
    for z in range(NZ):
        part = slice(z * plane, (z + 1) * plane)
        down[part, :main] = weights_ref[:, z, :, first : first + main].reshape(plane, main)
        down[part, main:] = weights_ref[:, z, :, tail:end].reshape(plane, end - tail)
    half = hidden.shape[0] // 2
    keep_ref[...] = dot_rows(hidden[:half], down[...])
    give_ref[...] = dot_rows(hidden[half:], down[...])


def grads_pass(normed, back, gate, up, hidden, weights):
    tokens, width = normed.shape
    units = hidden.shape[1]
    block = width // NX
    column = lambda i: (0, i)
    whole = lambda i: (0, 0)
    half = jax.ShapeDtypeStruct((tokens // 2, width), jnp.float32)
    packed_block = pl.BlockSpec((NY,) + weights.shape[1:], lambda i: (i, 0, 0, 0))
    return pl.pallas_call(
        grads_kernel,
        grid=(NX,),
        in_specs=[
            pl.BlockSpec((tokens, block), column),
            pl.BlockSpec((tokens, block), column),
            pl.BlockSpec((tokens, units), whole),
            pl.BlockSpec((tokens, units), whole),
            pl.BlockSpec((tokens, units), whole),
            packed_block,
        ],
        out_specs=[
            packed_block,
            pl.BlockSpec((tokens // 2, block), column),
            pl.BlockSpec((tokens // 2, block), column),
        ],
        out_shape=[jax.ShapeDtypeStruct(weights.shape, jnp.bfloat16), half, half],
        scratch_shapes=[pltpu.VMEM((block, units), jnp.bfloat16)],
        compiler_params=pltpu.CompilerParams(vmem_limit_bytes=VMEM_BYTES),
        cost_estimate=pl.CostEstimate(
            flops=8 * tokens * width * units,
            bytes_accessed=14 * tokens * width,
            transcendentals=0,
        ),
        name="grads_pass",
    )(normed, back, gate, up, hidden, weights)


def mixer_kernel(
    branch_ref,
    weights_ref,
    projected_ref,
    masks_ref,
    taps_ref,
    gated_ref,
    scale_ref,
    branch_part_ref,
    weights_part_ref,
    normed_ref,
    tokens_ref,
    grads_ref,
    back_ref,
    gain_ref,
    conv_ref,
    held,
):
    channels = gated_ref.shape[1]
    rows = grads_ref.shape[2]

    @pl.when(pl.program_id(0) == 0)
    def _():
        count = branch_ref.shape[0]
        back = dot_plain(branch_ref[...], weights_ref[:, 3 * channels : 4 * channels])
        b_part = projected_ref[:, :channels]
        c_part = projected_ref[:, channels : 2 * channels]
        x_part = projected_ref[:, 2 * channels :]
        tap_zero, tap_one, tap_two = taps_ref[0:1], taps_ref[1:2], taps_ref[2:3]
        one, two = masks_ref[:, 0:1] > 0.0, masks_ref[:, 1:2] > 0.0
        product = b_part * x_part
        first = jnp.where(one, pltpu.roll(product, 1, 0), 0.0)
        second = jnp.where(two, pltpu.roll(product, 2, 0), 0.0)
        conv_sum = tap_zero * product + tap_one * first + tap_two * second
        grad = back * c_part
        conv_ref[0:1] = jnp.sum(grad * product, axis=0, keepdims=True)
        conv_ref[1:2] = jnp.sum(grad * first, axis=0, keepdims=True)
        conv_ref[2:3] = jnp.sum(grad * second, axis=0, keepdims=True)
        back_product = tap_zero * grad
        back_product += tap_one * pltpu.roll(jnp.where(one, grad, 0.0), count - 1, 0)
        back_product += tap_two * pltpu.roll(jnp.where(two, grad, 0.0), count - 2, 0)
        held[:, :channels] = low(back_product * x_part)
        held[:, channels : 2 * channels] = low(back * conv_sum)
        held[:, 2 * channels :] = low(back_product * b_part)

    back_projected = held[...]
    plane = NY * rows
    grad_in = low(dot_columns(normed_ref[...], back_projected))
    grad_out = low(dot_columns(branch_part_ref[...], gated_ref[...]))
    for z in range(NZ):
        part = slice(z * plane, (z + 1) * plane)
        grads_ref[:, z, :, : 3 * channels] = grad_in[part].reshape(NY, rows, 3 * channels)
        grads_ref[:, z, :, 3 * channels :] = grad_out[part].reshape(NY, rows, channels)
    back_normed = dot_rows(back_projected, weights_part_ref[:, : 3 * channels])
    back_ref[...] = back_normed
    unit = tokens_ref[...].astype(jnp.float32) * scale_ref[...]
    gain_ref[...] = jnp.sum(back_normed * unit, axis=0, keepdims=True)


def mixer_pass(branch, weights, projected, masks, taps, gated, scale, normed, tokens):
    count, width = branch.shape
    channels = gated.shape[1]
    rows = width // N_DP
    block = width // NX
    whole = lambda i: (0, 0)
    column = pl.BlockSpec((count, block), lambda i: (0, i))
    return pl.pallas_call(
        mixer_kernel,
        grid=(NX,),
        in_specs=[
            pl.BlockSpec(branch.shape, whole),
            pl.BlockSpec(weights.shape, whole),
            pl.BlockSpec(projected.shape, whole),
            pl.BlockSpec(masks.shape, whole),
            pl.BlockSpec(taps.shape, whole),
            pl.BlockSpec(gated.shape, whole),
            pl.BlockSpec(scale.shape, whole),
            column,
            pl.BlockSpec((block, weights.shape[1]), lambda i: (i, 0)),
            column,
            column,
        ],
        out_specs=[
            pl.BlockSpec((NY, NZ, rows, 4 * channels), lambda i: (i, 0, 0, 0)),
            column,
            pl.BlockSpec((1, block), lambda i: (0, i)),
            pl.BlockSpec(taps.shape, whole),
        ],
        out_shape=[
            jax.ShapeDtypeStruct((NX * NY, NZ, rows, 4 * channels), jnp.bfloat16),
            jax.ShapeDtypeStruct((count, width), jnp.float32),
            jax.ShapeDtypeStruct((1, width), jnp.float32),
            jax.ShapeDtypeStruct(taps.shape, jnp.float32),
        ],
        scratch_shapes=[pltpu.VMEM((count, 3 * channels), jnp.bfloat16)],
        compiler_params=pltpu.CompilerParams(vmem_limit_bytes=VMEM_BYTES),
        cost_estimate=pl.CostEstimate(
            flops=16 * count * width * channels,
            bytes_accessed=20 * count * width,
            transcendentals=0,
        ),
        name="mixer_pass",
    )(branch, weights, projected, masks, taps, gated, scale, branch, weights, normed, tokens)


def pieces(value):
    high = lax.reduce_precision(value, 8, 7)
    rest = value - high
    middle = lax.reduce_precision(rest, 8, 7)
    return [low(high), low(middle), low(rest - middle)]


def shards(
    tokens_in,
    cotangent,
    segment_ids,
    in_weight,
    out_weight,
    gate_up_weight,
    down_weight,
    conv_weight,
    norm_gains,
    in_first,
    in_second,
    out_first,
    out_second,
    gate_up_first,
    gate_up_second,
    down_first,
    down_second,
    conv_first,
    conv_second,
    gains_first,
    gains_second,
):
    rows, length, width = tokens_in.shape
    count = rows * length
    taps_n, channels = conv_weight.shape
    units = gate_up_weight.shape[2]
    own_rows = gate_up_weight.shape[1]
    part_units = units // NZ
    core = lax.axis_index("tensor") % 2
    near = (lax.axis_index("dp") // NY) % NZ

    mix_cols = 4 * channels
    low_mix = jnp.concatenate(
        [
            in_weight[0],
            in_weight[1],
            in_weight[2],
            out_weight.T,
            jnp.pad(norm_gains.T, ((0, 0), (0, 126))),
        ],
        axis=1,
    )
    low_mix = low(low_mix)
    low_mix = jnp.stack(in_order(low_mix, swap_near(low_mix), near), axis=0)
    low_mix, gate_up_early, down_early, cotangent, tokens_in, segment_ids = (
        lax.optimization_barrier(
            (low_mix, gate_up_weight, down_weight, cotangent, tokens_in, segment_ids)
        )
    )
    low_ffn = low(jnp.concatenate([gate_up_early, down_early.T[None]], axis=0))
    keep = packed(lax.dynamic_slice_in_dim(low_ffn, near * part_units, part_units, 2))
    give = packed(lax.dynamic_slice_in_dim(low_ffn, (1 - near) * part_units, part_units, 2))
    take = swap_near(give)
    low_ffn = jnp.stack(in_order(keep, take, near), axis=0)
    ffn_copies = jnp.broadcast_to(low_ffn[None], (NX * NY,) + low_ffn.shape)
    back_out = cotangent.reshape(count, width)
    back_own, back_other = halves(back_out, core)
    back_near = swap_near(back_own)
    back_four = jnp.concatenate([back_own, back_near, back_other, swap_core(back_near)], axis=0)

    flat = wide(tokens_in.reshape(count, width))
    flat_half = halves(flat, core)[0]
    seg_flat = segment_ids.reshape(count)
    place = lax.iota(jnp.int32, count) % length
    mask_one = ((place >= 1) & (seg_flat == jnp.roll(seg_flat, 1)))[:, None]
    mask_two = ((place >= 2) & (seg_flat == jnp.roll(seg_flat, 2)))[:, None]
    masks = wide(jnp.concatenate([mask_one, mask_two], axis=1))
    scale_one = lax.rsqrt(jnp.mean(flat * flat, axis=-1, keepdims=True) + epsilon_norm)

    mix_full = exchange(jnp.broadcast_to(low_mix[None], (NX * NY,) + low_mix.shape))
    mix_full, ffn_copies, back_four, masks, scale_one = lax.optimization_barrier(
        (mix_full, ffn_copies, back_four, masks, scale_one)
    )
    ffn_full = exchange(ffn_copies)
    mix_full = mix_full.reshape(NX, NY, NZ, own_rows, -1).transpose(0, 2, 1, 3, 4).reshape(width, -1)
    in_full = mix_full[:, : 3 * channels]
    out_full = mix_full[:, 3 * channels : mix_cols]
    gains_value = wide(mix_full[:, mix_cols : mix_cols + 2]).T


    def mixer_local(projected, taps):
        product = projected[:, :channels] * projected[:, 2 * channels :]
        conv_sum = taps[0] * product + taps[1] * jnp.where(
            mask_one, jnp.roll(product, 1, axis=0), 0.0
        )
        conv_sum = conv_sum + taps[2] * jnp.where(mask_two, jnp.roll(product, 2, axis=0), 0.0)
        return projected[:, channels : 2 * channels] * conv_sum

    normed_one = low(rms_gain(flat, gains_value[0]))
    projected = product_of("td,dc->tc", normed_one, in_full)
    gated = low(mixer_local(projected, conv_weight))
    middle = flat_half + sum_four(product_of("tc,dc->td", gated, out_full), core)
    normed_two_f, norm_two_pull = jax.vjp(rms_gain, middle, gains_value[1])
    normed_two = low(normed_two_f)
    normed_two = jnp.concatenate([normed_two, swap_near(normed_two)], axis=0)
    normed_two, ffn_full = lax.optimization_barrier((normed_two, ffn_full))
    normed_two = jnp.concatenate([normed_two, swap_core(normed_two)], axis=0)

    back_gate, back_up, hidden, back_keep, back_give = hidden_pass(
        normed_two, back_four, ffn_full
    )
    back_pair = back_keep + swap_core(back_give)
    back_pair, back_gate, back_up, hidden = lax.optimization_barrier(
        (back_pair, back_gate, back_up, hidden)
    )
    grad_ffn, ffn_keep, ffn_give = grads_pass(
        normed_two, back_four, back_gate, back_up, hidden, ffn_full
    )
    back_normed_two = back_pair[: count // 2] + wide(swap_near(low(back_pair[count // 2 :])))
    back_normed_two, grad_ffn = lax.optimization_barrier((back_normed_two, grad_ffn))
    back_normed_two = across_high(back_normed_two)
    grad_ffn = exchange(grad_ffn)

    ffn_keep, ffn_give, back_normed_two = lax.optimization_barrier(
        (ffn_keep, ffn_give, back_normed_two)
    )
    ffn_pair = ffn_keep + swap_core(ffn_give)
    ffn_half = ffn_pair[: count // 2] + wide(swap_near(low(ffn_pair[count // 2 :])))

    back_middle_norm, grad_gain_two = norm_two_pull(back_normed_two)
    back_middle = wide(back_own) + back_middle_norm
    back_branch = low(back_middle)
    back_branch = joined(back_branch, swap_core(back_branch), core)
    grad_mix, back_normed_one, grad_gain_one, grad_conv = mixer_pass(
        back_branch,
        mix_full,
        projected,
        masks,
        conv_weight,
        gated,
        scale_one,
        normed_one,
        tokens_in.reshape(count, width),
    )
    grad_gains = jnp.concatenate([grad_gain_one, 0.5 * grad_gain_two[None]], axis=0)
    grad_gains = grad_gains.reshape(2, N_DP, own_rows).transpose(1, 0, 2).reshape(N_DP, -1)
    grad_conv = jnp.broadcast_to(grad_conv.reshape(1, -1), (N_DP, grad_conv.size))
    small_size = grad_gains.shape[1] + grad_conv.shape[1]
    small = jnp.concatenate([grad_gains, grad_conv], axis=1)
    small = jnp.pad(small, ((0, 0), (0, 1024 - small_size))).reshape(N_DP, 8, 128)
    small = jnp.concatenate(
        pieces(small) + [jnp.zeros((N_DP, own_rows - 24, 128), jnp.bfloat16)], axis=1
    )
    grad_mix = jnp.concatenate([grad_mix, to_planes(small.reshape(width, 128))], axis=3)
    own, other = halves(back_normed_one, core)
    back_normed_one = own + swap_core(other)
    grad_ffn, grad_mix, back_normed_one = lax.optimization_barrier(
        (grad_ffn, grad_mix, back_normed_one)
    )
    red_mix = jnp.sum(wide(exchange(grad_mix)), axis=0)
    keep = lax.dynamic_index_in_dim(red_mix, near, 0, keepdims=False)
    red_mix = keep + swap_near(lax.dynamic_index_in_dim(red_mix, 1 - near, 0, keepdims=False))
    back_normed_one = across_high(back_normed_one)
    grad_ffn, back_normed_one, ffn_half = lax.optimization_barrier(
        (grad_ffn, back_normed_one, ffn_half)
    )
    red_ffn = whole_units(jnp.sum(wide(grad_ffn), axis=0), near)
    result = middle + across_high(ffn_half)
    result = joined(result, swap_core(result), core)
    back_tokens_norm = jax.vjp(rms_gain, flat_half, gains_value[0])[1](back_normed_one)[0]
    back_tokens = back_middle + back_tokens_norm
    back_tokens = joined(back_tokens, swap_core(back_tokens), core)

    red_small = jnp.sum(red_mix[:24, mix_cols:].reshape(3, 1024), axis=0)
    red_gains = red_small[: norm_gains.size].reshape(norm_gains.shape)
    red_gains = jnp.sum(lax.all_gather(red_gains, "tensor"), axis=0)
    conv_total = red_small[norm_gains.size : small_size].reshape(conv_weight.shape)
    red_in = red_mix[:, : 3 * channels].reshape(-1, 3, channels).transpose(1, 0, 2)
    red_out = red_mix[:, 3 * channels : mix_cols].T
    red_gate_up = red_ffn[:2]
    red_down = red_ffn[2].T
    rate_wide = 0.8 / D**0.5
    rate_down = 0.8 / FF**0.5
    in_new = adam_step(in_weight, red_in, in_first, in_second, rate_wide, 0.1)
    out_new = adam_step(out_weight, red_out, out_first, out_second, rate_wide, 0.1)
    gate_up_new = adam_step(
        gate_up_weight, red_gate_up, gate_up_first, gate_up_second, rate_wide, 0.1
    )
    down_new = adam_step(down_weight, red_down, down_first, down_second, rate_down, 0.1)
    conv_new = adam_step(conv_weight, conv_total, conv_first, conv_second, 1.0, 0.0)
    gains_new = adam_step(norm_gains, red_gains, gains_first, gains_second, 0.3, 0.0)
    return (
        result.reshape(rows, length, width),
        back_tokens.reshape(rows, length, width),
        in_new[0],
        in_new[1],
        in_new[2],
        out_new[0],
        out_new[1],
        out_new[2],
        gate_up_new[0],
        gate_up_new[1],
        gate_up_new[2],
        down_new[0],
        down_new[1],
        down_new[2],
        conv_new[0],
        conv_new[1],
        conv_new[2],
        gains_new[0],
        gains_new[1],
        gains_new[2],
    )


def solution(mesh):
    in_specs = (
        P("dp", None, None),
        P("dp", None, None),
        P("dp", None),
        P(None, "dp", "tensor"),
        P("tensor", "dp"),
        P(None, "dp", "tensor"),
        P("tensor", "dp"),
        P(None, "tensor"),
        P(None, "dp"),
        P(None, "dp", "tensor"),
        P(None, "dp", "tensor"),
        P("tensor", "dp"),
        P("tensor", "dp"),
        P(None, "dp", "tensor"),
        P(None, "dp", "tensor"),
        P("tensor", "dp"),
        P("tensor", "dp"),
        P(None, "tensor"),
        P(None, "tensor"),
        P(None, "dp"),
        P(None, "dp"),
    )
    out_specs = (
        P("dp", None, None),
        P("dp", None, None),
        P(None, "dp", "tensor"),
        P(None, "dp", "tensor"),
        P(None, "dp", "tensor"),
        P("tensor", "dp"),
        P("tensor", "dp"),
        P("tensor", "dp"),
        P(None, "dp", "tensor"),
        P(None, "dp", "tensor"),
        P(None, "dp", "tensor"),
        P("tensor", "dp"),
        P("tensor", "dp"),
        P("tensor", "dp"),
        P(None, "tensor"),
        P(None, "tensor"),
        P(None, "tensor"),
        P(None, "dp"),
        P(None, "dp"),
        P(None, "dp"),
    )
    return jax.shard_map(shards, mesh=mesh, in_specs=in_specs, out_specs=out_specs, check_vma=False)
```

```python
import jax
import jax.numpy as jnp
from jax import lax
from jax.experimental import pallas as pl
from jax.experimental.pallas import tpu as pltpu
from jax.sharding import PartitionSpec as P

D = 1024
FF = 4608
ADAM_STEP = 10
NX, NZ, NY = 4, 2, 4
N_DP = NX * NZ * NY
NEAR_PAIRS = [(d, d ^ NY) for d in range(N_DP)]
PLANES = [[(x * NZ + z) * NY + y for x in range(NX) for y in range(NY)] for z in range(NZ)]
CORE_PAIRS = [(0, 1), (1, 0), (2, 3), (3, 2)]
HIGH_PAIRS = [(0, 2), (2, 0), (1, 3), (3, 1)]


epsilon_norm = 1e-05
epsilon_adam = 1e-08
beta_one = 0.9
beta_two = 0.95


def rms_gain(values, gain_row):
    return (
        values
        * lax.rsqrt(jnp.mean(values * values, axis=-1, keepdims=True) + epsilon_norm)
        * gain_row
    )


def adam_step(master, gradient, first, second, step_rate, decay_rate):
    first_new = beta_one * first + (1.0 - beta_one) * gradient
    second_new = beta_two * second + (1.0 - beta_two) * gradient * gradient
    first_hat = first_new / (1.0 - beta_one**ADAM_STEP)
    second_hat = second_new / (1.0 - beta_two**ADAM_STEP)
    master_new = master - step_rate * (
        first_hat / (jnp.sqrt(second_hat) + epsilon_adam) + decay_rate * master
    )
    return (master_new, first_new, second_new)


def swap_core(value):
    return lax.ppermute(value, "tensor", CORE_PAIRS)


def swap_high(value):
    return lax.ppermute(value, "tensor", HIGH_PAIRS)


def swap_near(value):
    return lax.ppermute(value, "dp", NEAR_PAIRS)


def low(value):
    return value.astype(jnp.bfloat16)


def wide(value):
    return value.astype(jnp.float32)


def product_of(spec, left, right):
    return jnp.einsum(spec, left, right, preferred_element_type=jnp.float32)


def halves(value, core):
    half = value.shape[0] // 2
    return (
        lax.dynamic_slice_in_dim(value, core * half, half, 0),
        lax.dynamic_slice_in_dim(value, (1 - core) * half, half, 0),
    )


def joined(own, other, core):
    first = core == 0
    return jnp.concatenate([jnp.where(first, own, other), jnp.where(first, other, own)], axis=0)


def across_high(value):
    value = low(value)
    return wide(value) + wide(swap_high(value))


def sum_four(part, core):
    own, other = halves(part, core)
    return across_high(own + swap_core(other))


def to_planes(grad):
    columns = grad.shape[1]
    blocks = grad.reshape(NX, NZ, NY, -1, columns).transpose(0, 2, 1, 3, 4)
    return blocks.reshape(NX * NY, NZ, -1, columns)


def exchange(blocks):
    return lax.all_to_all(blocks, "dp", 0, 0, tiled=True, axis_index_groups=PLANES)


def in_order(mine, theirs, near):
    first = near == 0
    return jnp.where(first, mine, theirs), jnp.where(first, theirs, mine)


def places(units):
    main = units // 128 * 128
    rest = units - main
    return main, [(k * main, 3 * main + k * rest, 3 * main + (k + 1) * rest) for k in range(3)]


def packed(three):
    main = places(three.shape[2])[0]
    parts = [three[k, :, :main] for k in range(3)] + [three[k, :, main:] for k in range(3)]
    return jnp.concatenate(parts, axis=1)


def unpacked(rows):
    main, where = places(rows.shape[1] // 3)
    return jnp.stack(
        [
            jnp.concatenate([rows[:, start : start + main], rows[:, tail:end]], axis=1)
            for start, tail, end in where
        ]
    )


def whole_units(grad, near):
    keep = lax.dynamic_index_in_dim(grad, near, 0, keepdims=False)
    take = swap_near(lax.dynamic_index_in_dim(grad, 1 - near, 0, keepdims=False))
    return jnp.concatenate(in_order(unpacked(keep), unpacked(take), near), axis=2)


def spread_kernel(block_ref, copies_ref, sems):
    copies = [
        pltpu.make_async_copy(block_ref, copies_ref.at[i], sems.at[i]) for i in range(NX * NY)
    ]
    for copy in copies:
        copy.start()
    for copy in copies:
        copy.wait()


def spread_pass(block):
    return pl.pallas_call(
        spread_kernel,
        in_specs=[pl.BlockSpec(memory_space=pltpu.VMEM)],
        out_specs=pl.BlockSpec(memory_space=pltpu.HBM),
        out_shape=jax.ShapeDtypeStruct((NX * NY,) + block.shape, block.dtype),
        scratch_shapes=[pltpu.SemaphoreType.DMA((NX * NY,))],
        cost_estimate=pl.CostEstimate(
            flops=0, bytes_accessed=2 * NX * NY * block.size, transcendentals=0
        ),
        name="spread_pass",
    )(block)


VMEM_BYTES = 40 * 1024 * 1024


def dot_rows(left, right):
    return lax.dot_general(left, right, (((1,), (1,)), ((), ())), preferred_element_type=jnp.float32)


def dot_columns(left, right):
    return lax.dot_general(left, right, (((0,), (0,)), ((), ())), preferred_element_type=jnp.float32)


def dot_plain(left, right):
    return jnp.dot(left, right, preferred_element_type=jnp.float32)


def hidden_kernel(
    normed_ref, back_ref, weights_ref, gate_ref, up_ref, hidden_ref, keep_ref, give_ref, held
):
    step = pl.program_id(0)
    rows = weights_ref.shape[2]
    main, where = places(gate_ref.shape[1])

    @pl.when(step == 0)
    def _():
        for x in range(NX):
            for z in range(NZ):
                for y in range(NY):
                    start = ((x * NZ + z) * NY + y) * rows
                    for k, (first, tail, end) in enumerate(where):
                        block = weights_ref.at[x * NY + y, z]
                        held[k, start : start + rows, :main] = block[:, first : first + main]
                        held[k, start : start + rows, main:] = block[:, tail:end]

    normed = normed_ref[...]
    gate = dot_plain(normed, held[0])
    up = dot_plain(normed, held[1])
    back = dot_plain(back_ref[...], held[2])
    share = jax.nn.sigmoid(gate)
    smooth = gate * share
    hidden_ref[...] = low(smooth * up)
    back_up = low(back * smooth)
    back_gate = low(back * up * (share + smooth * (1.0 - share)))
    gate_ref[...] = back_gate
    up_ref[...] = back_up
    part = dot_rows(back_gate, held[0]) + dot_rows(back_up, held[1])

    @pl.when(step < 2)
    def _():
        give_ref[...] = part

    @pl.when(step >= 2)
    def _():
        keep_ref[...] = part


def hidden_pass(normed, back, weights):
    tokens, width = normed.shape
    units = weights.shape[-1] // 3
    block = tokens // 4
    turned = lambda i: ((i + 2) % 4, 0)
    narrow = jax.ShapeDtypeStruct((tokens, units), jnp.bfloat16)
    half = jax.ShapeDtypeStruct((tokens // 2, width), jnp.float32)
    return pl.pallas_call(
        hidden_kernel,
        grid=(4,),
        in_specs=[
            pl.BlockSpec((block, width), turned),
            pl.BlockSpec((block, width), turned),
            pl.BlockSpec(weights.shape, lambda i: (0, 0, 0, 0)),
        ],
        out_specs=[
            pl.BlockSpec((block, units), turned),
            pl.BlockSpec((block, units), turned),
            pl.BlockSpec((block, units), turned),
            pl.BlockSpec((block, width), lambda i: (jnp.maximum(i - 2, 0), 0)),
            pl.BlockSpec((block, width), lambda i: (jnp.minimum(i, 1), 0)),
        ],
        out_shape=[narrow, narrow, narrow, half, half],
        scratch_shapes=[pltpu.VMEM((3, width, units), jnp.bfloat16)],
        compiler_params=pltpu.CompilerParams(vmem_limit_bytes=VMEM_BYTES),
        cost_estimate=pl.CostEstimate(
            flops=10 * tokens * width * units,
            bytes_accessed=16 * tokens * width,
            transcendentals=tokens * units,
        ),
        name="hidden_pass",
    )(normed, back, weights)


def grads_kernel(
    normed_ref,
    back_ref,
    gate_ref,
    up_ref,
    hidden_ref,
    weights_ref,
    grads_ref,
    keep_ref,
    give_ref,
    down,
):
    rows = weights_ref.shape[2]
    units = hidden_ref.shape[1]
    plane = NY * rows
    main, where = places(units)
    normed, hidden = normed_ref[...], hidden_ref[...]
    pairs = ((normed, gate_ref[...]), (normed, up_ref[...]), (back_ref[...], hidden))
    for (left, right), (first, tail, end) in zip(pairs, where):
        grad = low(dot_columns(left, right))
        for z in range(NZ):
            part = grad[z * plane : (z + 1) * plane]
            grads_ref[:, z, :, first : first + main] = part[:, :main].reshape(NY, rows, main)
            grads_ref[:, z, :, tail:end] = part[:, main:].reshape(NY, rows, end - tail)
    first, tail, end = where[2]
    for z in range(NZ):
        part = slice(z * plane, (z + 1) * plane)
        down[part, :main] = weights_ref[:, z, :, first : first + main].reshape(plane, main)
        down[part, main:] = weights_ref[:, z, :, tail:end].reshape(plane, end - tail)
    half = hidden.shape[0] // 2
    keep_ref[...] = dot_rows(hidden[:half], down[...])
    give_ref[...] = dot_rows(hidden[half:], down[...])


def grads_pass(normed, back, gate, up, hidden, weights):
    tokens, width = normed.shape
    units = hidden.shape[1]
    block = width // NX
    column = lambda i: (0, i)
    whole = lambda i: (0, 0)
    half = jax.ShapeDtypeStruct((tokens // 2, width), jnp.float32)
    packed_block = pl.BlockSpec((NY,) + weights.shape[1:], lambda i: (i, 0, 0, 0))
    return pl.pallas_call(
        grads_kernel,
        grid=(NX,),
        in_specs=[
            pl.BlockSpec((tokens, block), column),
            pl.BlockSpec((tokens, block), column),
            pl.BlockSpec((tokens, units), whole),
            pl.BlockSpec((tokens, units), whole),
            pl.BlockSpec((tokens, units), whole),
            packed_block,
        ],
        out_specs=[
            packed_block,
            pl.BlockSpec((tokens // 2, block), column),
            pl.BlockSpec((tokens // 2, block), column),
        ],
        out_shape=[jax.ShapeDtypeStruct(weights.shape, jnp.bfloat16), half, half],
        scratch_shapes=[pltpu.VMEM((block, units), jnp.bfloat16)],
        compiler_params=pltpu.CompilerParams(vmem_limit_bytes=VMEM_BYTES),
        cost_estimate=pl.CostEstimate(
            flops=8 * tokens * width * units,
            bytes_accessed=14 * tokens * width,
            transcendentals=0,
        ),
        name="grads_pass",
    )(normed, back, gate, up, hidden, weights)


def mixer_kernel(
    branch_ref,
    weights_ref,
    projected_ref,
    masks_ref,
    taps_ref,
    gated_ref,
    scale_ref,
    branch_part_ref,
    weights_part_ref,
    normed_ref,
    tokens_ref,
    grads_ref,
    back_ref,
    gain_ref,
    conv_ref,
    held,
):
    channels = gated_ref.shape[1]
    rows = grads_ref.shape[2]

    @pl.when(pl.program_id(0) == 0)
    def _():
        count = branch_ref.shape[0]
        back = dot_plain(branch_ref[...], weights_ref[:, 3 * channels : 4 * channels])
        b_part = projected_ref[:, :channels]
        c_part = projected_ref[:, channels : 2 * channels]
        x_part = projected_ref[:, 2 * channels :]
        tap_zero, tap_one, tap_two = taps_ref[0:1], taps_ref[1:2], taps_ref[2:3]
        one, two = masks_ref[:, 0:1] > 0.0, masks_ref[:, 1:2] > 0.0
        product = b_part * x_part
        first = jnp.where(one, pltpu.roll(product, 1, 0), 0.0)
        second = jnp.where(two, pltpu.roll(product, 2, 0), 0.0)
        conv_sum = tap_zero * product + tap_one * first + tap_two * second
        grad = back * c_part
        conv_ref[0:1] = jnp.sum(grad * product, axis=0, keepdims=True)
        conv_ref[1:2] = jnp.sum(grad * first, axis=0, keepdims=True)
        conv_ref[2:3] = jnp.sum(grad * second, axis=0, keepdims=True)
        back_product = tap_zero * grad
        back_product += tap_one * pltpu.roll(jnp.where(one, grad, 0.0), count - 1, 0)
        back_product += tap_two * pltpu.roll(jnp.where(two, grad, 0.0), count - 2, 0)
        held[:, :channels] = low(back_product * x_part)
        held[:, channels : 2 * channels] = low(back * conv_sum)
        held[:, 2 * channels :] = low(back_product * b_part)

    back_projected = held[...]
    plane = NY * rows
    grad_in = low(dot_columns(normed_ref[...], back_projected))
    grad_out = low(dot_columns(branch_part_ref[...], gated_ref[...]))
    for z in range(NZ):
        part = slice(z * plane, (z + 1) * plane)
        grads_ref[:, z, :, : 3 * channels] = grad_in[part].reshape(NY, rows, 3 * channels)
        grads_ref[:, z, :, 3 * channels :] = grad_out[part].reshape(NY, rows, channels)
    back_normed = dot_rows(back_projected, weights_part_ref[:, : 3 * channels])
    back_ref[...] = back_normed
    unit = tokens_ref[...].astype(jnp.float32) * scale_ref[...]
    gain_ref[...] = jnp.sum(back_normed * unit, axis=0, keepdims=True)


def mixer_pass(branch, weights, projected, masks, taps, gated, scale, normed, tokens):
    count, width = branch.shape
    channels = gated.shape[1]
    rows = width // N_DP
    block = width // NX
    whole = lambda i: (0, 0)
    column = pl.BlockSpec((count, block), lambda i: (0, i))
    return pl.pallas_call(
        mixer_kernel,
        grid=(NX,),
        in_specs=[
            pl.BlockSpec(branch.shape, whole),
            pl.BlockSpec(weights.shape, whole),
            pl.BlockSpec(projected.shape, whole),
            pl.BlockSpec(masks.shape, whole),
            pl.BlockSpec(taps.shape, whole),
            pl.BlockSpec(gated.shape, whole),
            pl.BlockSpec(scale.shape, whole),
            column,
            pl.BlockSpec((block, weights.shape[1]), lambda i: (i, 0)),
            column,
            column,
        ],
        out_specs=[
            pl.BlockSpec((NY, NZ, rows, 4 * channels), lambda i: (i, 0, 0, 0)),
            column,
            pl.BlockSpec((1, block), lambda i: (0, i)),
            pl.BlockSpec(taps.shape, whole),
        ],
        out_shape=[
            jax.ShapeDtypeStruct((NX * NY, NZ, rows, 4 * channels), jnp.bfloat16),
            jax.ShapeDtypeStruct((count, width), jnp.float32),
            jax.ShapeDtypeStruct((1, width), jnp.float32),
            jax.ShapeDtypeStruct(taps.shape, jnp.float32),
        ],
        scratch_shapes=[pltpu.VMEM((count, 3 * channels), jnp.bfloat16)],
        compiler_params=pltpu.CompilerParams(vmem_limit_bytes=VMEM_BYTES),
        cost_estimate=pl.CostEstimate(
            flops=16 * count * width * channels,
            bytes_accessed=20 * count * width,
            transcendentals=0,
        ),
        name="mixer_pass",
    )(branch, weights, projected, masks, taps, gated, scale, branch, weights, normed, tokens)


def pieces(value):
    high = lax.reduce_precision(value, 8, 7)
    rest = value - high
    middle = lax.reduce_precision(rest, 8, 7)
    return [low(high), low(middle), low(rest - middle)]


def shards(
    tokens_in,
    cotangent,
    segment_ids,
    in_weight,
    out_weight,
    gate_up_weight,
    down_weight,
    conv_weight,
    norm_gains,
    in_first,
    in_second,
    out_first,
    out_second,
    gate_up_first,
    gate_up_second,
    down_first,
    down_second,
    conv_first,
    conv_second,
    gains_first,
    gains_second,
):
    rows, length, width = tokens_in.shape
    count = rows * length
    taps_n, channels = conv_weight.shape
    units = gate_up_weight.shape[2]
    own_rows = gate_up_weight.shape[1]
    part_units = units // NZ
    core = lax.axis_index("tensor") % 2
    near = (lax.axis_index("dp") // NY) % NZ

    mix_cols = 4 * channels
    low_mix = jnp.concatenate(
        [
            in_weight[0],
            in_weight[1],
            in_weight[2],
            out_weight.T,
            jnp.pad(norm_gains.T, ((0, 0), (0, 126))),
        ],
        axis=1,
    )
    low_mix = low(low_mix)
    low_mix = jnp.stack(in_order(low_mix, swap_near(low_mix), near), axis=0)
    low_mix, gate_up_early, down_early, cotangent, tokens_in, segment_ids = (
        lax.optimization_barrier(
            (low_mix, gate_up_weight, down_weight, cotangent, tokens_in, segment_ids)
        )
    )
    low_ffn = low(jnp.concatenate([gate_up_early, down_early.T[None]], axis=0))
    keep = packed(lax.dynamic_slice_in_dim(low_ffn, near * part_units, part_units, 2))
    give = packed(lax.dynamic_slice_in_dim(low_ffn, (1 - near) * part_units, part_units, 2))
    take = swap_near(give)
    low_ffn = jnp.stack(in_order(keep, take, near), axis=0)
    ffn_copies = spread_pass(low_ffn)
    back_out = cotangent.reshape(count, width)
    back_own, back_other = halves(back_out, core)
    back_near = swap_near(back_own)
    back_twin = swap_core(back_near)

    flat = wide(tokens_in.reshape(count, width))
    flat_half = halves(flat, core)[0]
    seg_flat = segment_ids.reshape(count)
    place = lax.iota(jnp.int32, count) % length
    mask_one = ((place >= 1) & (seg_flat == jnp.roll(seg_flat, 1)))[:, None]
    mask_two = ((place >= 2) & (seg_flat == jnp.roll(seg_flat, 2)))[:, None]
    masks = wide(jnp.concatenate([mask_one, mask_two], axis=1))
    scale_one = lax.rsqrt(jnp.mean(flat * flat, axis=-1, keepdims=True) + epsilon_norm)

    mix_full = exchange(jnp.broadcast_to(low_mix[None], (NX * NY,) + low_mix.shape))
    mix_full, ffn_copies, back_near, back_twin = lax.optimization_barrier(
        (mix_full, ffn_copies, back_near, back_twin)
    )
    ffn_full = exchange(ffn_copies)
    mix_full = mix_full.reshape(NX, NY, NZ, own_rows, -1).transpose(0, 2, 1, 3, 4).reshape(width, -1)
    in_full = mix_full[:, : 3 * channels]
    out_full = mix_full[:, 3 * channels : mix_cols]
    gains_value = wide(mix_full[:, mix_cols : mix_cols + 2]).T


    def mixer_local(projected, taps):
        product = projected[:, :channels] * projected[:, 2 * channels :]
        conv_sum = taps[0] * product + taps[1] * jnp.where(
            mask_one, jnp.roll(product, 1, axis=0), 0.0
        )
        conv_sum = conv_sum + taps[2] * jnp.where(mask_two, jnp.roll(product, 2, axis=0), 0.0)
        return projected[:, channels : 2 * channels] * conv_sum

    normed_one = low(rms_gain(flat, gains_value[0]))
    projected = product_of("td,dc->tc", normed_one, in_full)
    gated = low(mixer_local(projected, conv_weight))
    middle = flat_half + sum_four(product_of("tc,dc->td", gated, out_full), core)
    normed_two_f, norm_two_pull = jax.vjp(rms_gain, middle, gains_value[1])
    normed_two = low(normed_two_f)
    normed_two = jnp.concatenate([normed_two, swap_near(normed_two)], axis=0)
    back_four = jnp.concatenate([back_own, back_near, back_other, back_twin], axis=0)
    normed_two, ffn_full, back_four, masks, scale_one = lax.optimization_barrier(
        (normed_two, ffn_full, back_four, masks, scale_one)
    )
    normed_two = jnp.concatenate([normed_two, swap_core(normed_two)], axis=0)

    back_gate, back_up, hidden, back_keep, back_give = hidden_pass(
        normed_two, back_four, ffn_full
    )
    back_pair = back_keep + swap_core(back_give)
    back_pair, back_gate, back_up, hidden = lax.optimization_barrier(
        (back_pair, back_gate, back_up, hidden)
    )
    grad_ffn, ffn_keep, ffn_give = grads_pass(
        normed_two, back_four, back_gate, back_up, hidden, ffn_full
    )
    back_normed_two = back_pair[: count // 2] + wide(swap_near(low(back_pair[count // 2 :])))
    back_normed_two, grad_ffn = lax.optimization_barrier((back_normed_two, grad_ffn))
    back_normed_two = across_high(back_normed_two)
    grad_ffn = exchange(grad_ffn)

    ffn_keep, ffn_give, back_normed_two = lax.optimization_barrier(
        (ffn_keep, ffn_give, back_normed_two)
    )
    ffn_pair = ffn_keep + swap_core(ffn_give)
    ffn_half = ffn_pair[: count // 2] + wide(swap_near(low(ffn_pair[count // 2 :])))

    back_middle_norm, grad_gain_two = norm_two_pull(back_normed_two)
    back_middle = wide(back_own) + back_middle_norm
    back_branch = low(back_middle)
    back_branch = joined(back_branch, swap_core(back_branch), core)
    grad_mix, back_normed_one, grad_gain_one, grad_conv = mixer_pass(
        back_branch,
        mix_full,
        projected,
        masks,
        conv_weight,
        gated,
        scale_one,
        normed_one,
        tokens_in.reshape(count, width),
    )
    grad_gains = jnp.concatenate([grad_gain_one, 0.5 * grad_gain_two[None]], axis=0)
    grad_gains = grad_gains.reshape(2, N_DP, own_rows).transpose(1, 0, 2).reshape(N_DP, -1)
    grad_conv = jnp.broadcast_to(grad_conv.reshape(1, -1), (N_DP, grad_conv.size))
    small_size = grad_gains.shape[1] + grad_conv.shape[1]
    small = jnp.concatenate([grad_gains, grad_conv], axis=1)
    small = jnp.pad(small, ((0, 0), (0, 1024 - small_size))).reshape(N_DP, 8, 128)
    small = jnp.concatenate(
        pieces(small) + [jnp.zeros((N_DP, own_rows - 24, 128), jnp.bfloat16)], axis=1
    )
    grad_mix = jnp.concatenate([grad_mix, to_planes(small.reshape(width, 128))], axis=3)
    own, other = halves(back_normed_one, core)
    back_normed_one = own + swap_core(other)
    grad_ffn, grad_mix, back_normed_one = lax.optimization_barrier(
        (grad_ffn, grad_mix, back_normed_one)
    )
    red_mix = jnp.sum(wide(exchange(grad_mix)), axis=0)
    keep = lax.dynamic_index_in_dim(red_mix, near, 0, keepdims=False)
    red_mix = keep + swap_near(lax.dynamic_index_in_dim(red_mix, 1 - near, 0, keepdims=False))
    back_normed_one = across_high(back_normed_one)
    grad_ffn, back_normed_one, ffn_half = lax.optimization_barrier(
        (grad_ffn, back_normed_one, ffn_half)
    )
    red_ffn = whole_units(jnp.sum(wide(grad_ffn), axis=0), near)
    result = middle + across_high(ffn_half)
    result = joined(result, swap_core(result), core)
    back_tokens_norm = jax.vjp(rms_gain, flat_half, gains_value[0])[1](back_normed_one)[0]
    back_tokens = back_middle + back_tokens_norm
    back_tokens = joined(back_tokens, swap_core(back_tokens), core)

    red_small = jnp.sum(red_mix[:24, mix_cols:].reshape(3, 1024), axis=0)
    red_gains = red_small[: norm_gains.size].reshape(norm_gains.shape)
    red_gains = jnp.sum(lax.all_gather(red_gains, "tensor"), axis=0)
    conv_total = red_small[norm_gains.size : small_size].reshape(conv_weight.shape)
    red_in = red_mix[:, : 3 * channels].reshape(-1, 3, channels).transpose(1, 0, 2)
    red_out = red_mix[:, 3 * channels : mix_cols].T
    red_gate_up = red_ffn[:2]
    red_down = red_ffn[2].T
    rate_wide = 0.8 / D**0.5
    rate_down = 0.8 / FF**0.5
    in_new = adam_step(in_weight, red_in, in_first, in_second, rate_wide, 0.1)
    out_new = adam_step(out_weight, red_out, out_first, out_second, rate_wide, 0.1)
    gate_up_new = adam_step(
        gate_up_weight, red_gate_up, gate_up_first, gate_up_second, rate_wide, 0.1
    )
    down_new = adam_step(down_weight, red_down, down_first, down_second, rate_down, 0.1)
    conv_new = adam_step(conv_weight, conv_total, conv_first, conv_second, 1.0, 0.0)
    gains_new = adam_step(norm_gains, red_gains, gains_first, gains_second, 0.3, 0.0)
    return (
        result.reshape(rows, length, width),
        back_tokens.reshape(rows, length, width),
        in_new[0],
        in_new[1],
        in_new[2],
        out_new[0],
        out_new[1],
        out_new[2],
        gate_up_new[0],
        gate_up_new[1],
        gate_up_new[2],
        down_new[0],
        down_new[1],
        down_new[2],
        conv_new[0],
        conv_new[1],
        conv_new[2],
        gains_new[0],
        gains_new[1],
        gains_new[2],
    )


def solution(mesh):
    in_specs = (
        P("dp", None, None),
        P("dp", None, None),
        P("dp", None),
        P(None, "dp", "tensor"),
        P("tensor", "dp"),
        P(None, "dp", "tensor"),
        P("tensor", "dp"),
        P(None, "tensor"),
        P(None, "dp"),
        P(None, "dp", "tensor"),
        P(None, "dp", "tensor"),
        P("tensor", "dp"),
        P("tensor", "dp"),
        P(None, "dp", "tensor"),
        P(None, "dp", "tensor"),
        P("tensor", "dp"),
        P("tensor", "dp"),
        P(None, "tensor"),
        P(None, "tensor"),
        P(None, "dp"),
        P(None, "dp"),
    )
    out_specs = (
        P("dp", None, None),
        P("dp", None, None),
        P(None, "dp", "tensor"),
        P(None, "dp", "tensor"),
        P(None, "dp", "tensor"),
        P("tensor", "dp"),
        P("tensor", "dp"),
        P("tensor", "dp"),
        P(None, "dp", "tensor"),
        P(None, "dp", "tensor"),
        P(None, "dp", "tensor"),
        P("tensor", "dp"),
        P("tensor", "dp"),
        P("tensor", "dp"),
        P(None, "tensor"),
        P(None, "tensor"),
        P(None, "tensor"),
        P(None, "dp"),
        P(None, "dp"),
        P(None, "dp"),
    )
    return jax.shard_map(shards, mesh=mesh, in_specs=in_specs, out_specs=out_specs, check_vma=False)
```

```python
import jax
import jax.numpy as jnp
from jax import lax
from jax.experimental import pallas as pl
from jax.experimental.pallas import tpu as pltpu
from jax.sharding import PartitionSpec as P

D = 1024
FF = 4608
ADAM_STEP = 10
NX, NZ, NY = 4, 2, 4
N_DP = NX * NZ * NY
NEAR_PAIRS = [(d, d ^ NY) for d in range(N_DP)]
PLANES = [[(x * NZ + z) * NY + y for x in range(NX) for y in range(NY)] for z in range(NZ)]
CORE_PAIRS = [(0, 1), (1, 0), (2, 3), (3, 2)]
HIGH_PAIRS = [(0, 2), (2, 0), (1, 3), (3, 1)]


epsilon_norm = 1e-05
epsilon_adam = 1e-08
beta_one = 0.9
beta_two = 0.95


def rms_gain(values, gain_row):
    return (
        values
        * lax.rsqrt(jnp.mean(values * values, axis=-1, keepdims=True) + epsilon_norm)
        * gain_row
    )


def adam_step(master, gradient, first, second, step_rate, decay_rate):
    first_new = beta_one * first + (1.0 - beta_one) * gradient
    second_new = beta_two * second + (1.0 - beta_two) * gradient * gradient
    first_hat = first_new / (1.0 - beta_one**ADAM_STEP)
    second_hat = second_new / (1.0 - beta_two**ADAM_STEP)
    master_new = master - step_rate * (
        first_hat / (jnp.sqrt(second_hat) + epsilon_adam) + decay_rate * master
    )
    return (master_new, first_new, second_new)


def swap_core(value):
    return lax.ppermute(value, "tensor", CORE_PAIRS)


def swap_high(value):
    return lax.ppermute(value, "tensor", HIGH_PAIRS)


def swap_near(value):
    return lax.ppermute(value, "dp", NEAR_PAIRS)


def low(value):
    return value.astype(jnp.bfloat16)


def wide(value):
    return value.astype(jnp.float32)


def product_of(spec, left, right):
    return jnp.einsum(spec, left, right, preferred_element_type=jnp.float32)


def halves(value, core):
    half = value.shape[0] // 2
    return (
        lax.dynamic_slice_in_dim(value, core * half, half, 0),
        lax.dynamic_slice_in_dim(value, (1 - core) * half, half, 0),
    )


def joined(own, other, core):
    first = core == 0
    return jnp.concatenate([jnp.where(first, own, other), jnp.where(first, other, own)], axis=0)


def across_high(value):
    value = low(value)
    return wide(value) + wide(swap_high(value))


def sum_four(part, core):
    own, other = halves(part, core)
    return across_high(own + swap_core(other))


def to_planes(grad):
    columns = grad.shape[1]
    blocks = grad.reshape(NX, NZ, NY, -1, columns).transpose(0, 2, 1, 3, 4)
    return blocks.reshape(NX * NY, NZ, -1, columns)


def exchange(blocks):
    return lax.all_to_all(blocks, "dp", 0, 0, tiled=True, axis_index_groups=PLANES)


def in_order(mine, theirs, near):
    first = near == 0
    return jnp.where(first, mine, theirs), jnp.where(first, theirs, mine)


def places(units):
    main = units // 128 * 128
    rest = units - main
    return main, [(k * main, 3 * main + k * rest, 3 * main + (k + 1) * rest) for k in range(3)]


def packed(three):
    main = places(three.shape[2])[0]
    parts = [three[k, :, :main] for k in range(3)] + [three[k, :, main:] for k in range(3)]
    return jnp.concatenate(parts, axis=1)


def unpacked(rows):
    main, where = places(rows.shape[1] // 3)
    return jnp.stack(
        [
            jnp.concatenate([rows[:, start : start + main], rows[:, tail:end]], axis=1)
            for start, tail, end in where
        ]
    )


def whole_units(grad, near):
    keep = lax.dynamic_index_in_dim(grad, near, 0, keepdims=False)
    take = swap_near(lax.dynamic_index_in_dim(grad, 1 - near, 0, keepdims=False))
    return jnp.concatenate(in_order(unpacked(keep), unpacked(take), near), axis=2)


def spread_kernel(block_ref, copies_ref, sems):
    copies = [
        pltpu.make_async_copy(block_ref, copies_ref.at[i], sems.at[i]) for i in range(NX * NY)
    ]
    for copy in copies:
        copy.start()
    for copy in copies:
        copy.wait()


def spread_pass(block):
    return pl.pallas_call(
        spread_kernel,
        in_specs=[pl.BlockSpec(memory_space=pltpu.VMEM)],
        out_specs=pl.BlockSpec(memory_space=pltpu.HBM),
        out_shape=jax.ShapeDtypeStruct((NX * NY,) + block.shape, block.dtype),
        scratch_shapes=[pltpu.SemaphoreType.DMA((NX * NY,))],
        cost_estimate=pl.CostEstimate(
            flops=0, bytes_accessed=2 * NX * NY * block.size, transcendentals=0
        ),
        name="spread_pass",
    )(block)


VMEM_BYTES = 40 * 1024 * 1024


def dot_rows(left, right):
    return lax.dot_general(left, right, (((1,), (1,)), ((), ())), preferred_element_type=jnp.float32)


def dot_columns(left, right):
    return lax.dot_general(left, right, (((0,), (0,)), ((), ())), preferred_element_type=jnp.float32)


def dot_plain(left, right):
    return jnp.dot(left, right, preferred_element_type=jnp.float32)


def hidden_kernel(
    normed_ref, back_ref, weights_ref, gate_ref, up_ref, hidden_ref, keep_ref, give_ref, held
):
    step = pl.program_id(0)
    rows = weights_ref.shape[2]
    main, where = places(gate_ref.shape[1])

    @pl.when(step == 0)
    def _():
        for x in range(NX):
            for z in range(NZ):
                for y in range(NY):
                    start = ((x * NZ + z) * NY + y) * rows
                    for k, (first, tail, end) in enumerate(where):
                        block = weights_ref.at[x * NY + y, z]
                        held[k, start : start + rows, :main] = block[:, first : first + main]
                        held[k, start : start + rows, main:] = block[:, tail:end]

    normed = normed_ref[...]
    gate = dot_plain(normed, held[0])
    up = dot_plain(normed, held[1])
    back = dot_plain(back_ref[...], held[2])
    share = jax.nn.sigmoid(gate)
    smooth = gate * share
    hidden_ref[...] = low(smooth * up)
    back_up = low(back * smooth)
    back_gate = low(back * up * (share + smooth * (1.0 - share)))
    gate_ref[...] = back_gate
    up_ref[...] = back_up
    part = dot_rows(back_gate, held[0]) + dot_rows(back_up, held[1])

    @pl.when(step < 2)
    def _():
        give_ref[...] = low(part)

    @pl.when(step >= 2)
    def _():
        keep_ref[...] = part


def hidden_pass(normed, back, weights):
    tokens, width = normed.shape
    units = weights.shape[-1] // 3
    block = tokens // 4
    turned = lambda i: ((i + 2) % 4, 0)
    narrow = jax.ShapeDtypeStruct((tokens, units), jnp.bfloat16)
    half = jax.ShapeDtypeStruct((tokens // 2, width), jnp.float32)
    return pl.pallas_call(
        hidden_kernel,
        grid=(4,),
        in_specs=[
            pl.BlockSpec((block, width), turned),
            pl.BlockSpec((block, width), turned),
            pl.BlockSpec(weights.shape, lambda i: (0, 0, 0, 0)),
        ],
        out_specs=[
            pl.BlockSpec((block, units), turned),
            pl.BlockSpec((block, units), turned),
            pl.BlockSpec((block, units), turned),
            pl.BlockSpec((block, width), lambda i: (jnp.maximum(i - 2, 0), 0)),
            pl.BlockSpec((block, width), lambda i: (jnp.minimum(i, 1), 0)),
        ],
        out_shape=[narrow, narrow, narrow, half, jax.ShapeDtypeStruct(half.shape, jnp.bfloat16)],
        scratch_shapes=[pltpu.VMEM((3, width, units), jnp.bfloat16)],
        compiler_params=pltpu.CompilerParams(vmem_limit_bytes=VMEM_BYTES),
        cost_estimate=pl.CostEstimate(
            flops=10 * tokens * width * units,
            bytes_accessed=16 * tokens * width,
            transcendentals=tokens * units,
        ),
        name="hidden_pass",
    )(normed, back, weights)


def grads_kernel(
    normed_ref,
    back_ref,
    gate_ref,
    up_ref,
    hidden_ref,
    weights_ref,
    grads_ref,
    keep_ref,
    give_ref,
    down,
):
    rows = weights_ref.shape[2]
    units = hidden_ref.shape[1]
    plane = NY * rows
    main, where = places(units)
    normed, hidden = normed_ref[...], hidden_ref[...]
    pairs = ((normed, gate_ref[...]), (normed, up_ref[...]), (back_ref[...], hidden))
    for (left, right), (first, tail, end) in zip(pairs, where):
        grad = low(dot_columns(left, right))
        for z in range(NZ):
            part = grad[z * plane : (z + 1) * plane]
            grads_ref[:, z, :, first : first + main] = part[:, :main].reshape(NY, rows, main)
            grads_ref[:, z, :, tail:end] = part[:, main:].reshape(NY, rows, end - tail)
    first, tail, end = where[2]
    for z in range(NZ):
        part = slice(z * plane, (z + 1) * plane)
        down[part, :main] = weights_ref[:, z, :, first : first + main].reshape(plane, main)
        down[part, main:] = weights_ref[:, z, :, tail:end].reshape(plane, end - tail)
    half = hidden.shape[0] // 2
    keep_ref[...] = dot_rows(hidden[:half], down[...])
    give_ref[...] = dot_rows(hidden[half:], down[...])


def grads_pass(normed, back, gate, up, hidden, weights):
    tokens, width = normed.shape
    units = hidden.shape[1]
    block = width // NX
    column = lambda i: (0, i)
    whole = lambda i: (0, 0)
    half = jax.ShapeDtypeStruct((tokens // 2, width), jnp.float32)
    packed_block = pl.BlockSpec((NY,) + weights.shape[1:], lambda i: (i, 0, 0, 0))
    return pl.pallas_call(
        grads_kernel,
        grid=(NX,),
        in_specs=[
            pl.BlockSpec((tokens, block), column),
            pl.BlockSpec((tokens, block), column),
            pl.BlockSpec((tokens, units), whole),
            pl.BlockSpec((tokens, units), whole),
            pl.BlockSpec((tokens, units), whole),
            packed_block,
        ],
        out_specs=[
            packed_block,
            pl.BlockSpec((tokens // 2, block), column),
            pl.BlockSpec((tokens // 2, block), column),
        ],
        out_shape=[jax.ShapeDtypeStruct(weights.shape, jnp.bfloat16), half, half],
        scratch_shapes=[pltpu.VMEM((block, units), jnp.bfloat16)],
        compiler_params=pltpu.CompilerParams(vmem_limit_bytes=VMEM_BYTES),
        cost_estimate=pl.CostEstimate(
            flops=8 * tokens * width * units,
            bytes_accessed=14 * tokens * width,
            transcendentals=0,
        ),
        name="grads_pass",
    )(normed, back, gate, up, hidden, weights)


def mixer_kernel(
    branch_ref,
    weights_ref,
    projected_ref,
    masks_ref,
    taps_ref,
    gated_ref,
    scale_ref,
    branch_part_ref,
    weights_part_ref,
    normed_ref,
    tokens_ref,
    grads_ref,
    back_ref,
    gain_ref,
    conv_ref,
    held,
):
    channels = gated_ref.shape[1]
    rows = grads_ref.shape[2]

    @pl.when(pl.program_id(0) == 0)
    def _():
        count = branch_ref.shape[0]
        back = dot_plain(branch_ref[...], weights_ref[:, 3 * channels : 4 * channels])
        b_part = projected_ref[:, :channels]
        c_part = projected_ref[:, channels : 2 * channels]
        x_part = projected_ref[:, 2 * channels :]
        tap_zero, tap_one, tap_two = taps_ref[0:1], taps_ref[1:2], taps_ref[2:3]
        one, two = masks_ref[:, 0:1] > 0.0, masks_ref[:, 1:2] > 0.0
        product = b_part * x_part
        first = jnp.where(one, pltpu.roll(product, 1, 0), 0.0)
        second = jnp.where(two, pltpu.roll(product, 2, 0), 0.0)
        conv_sum = tap_zero * product + tap_one * first + tap_two * second
        grad = back * c_part
        conv_ref[0:1] = jnp.sum(grad * product, axis=0, keepdims=True)
        conv_ref[1:2] = jnp.sum(grad * first, axis=0, keepdims=True)
        conv_ref[2:3] = jnp.sum(grad * second, axis=0, keepdims=True)
        back_product = tap_zero * grad
        back_product += tap_one * pltpu.roll(jnp.where(one, grad, 0.0), count - 1, 0)
        back_product += tap_two * pltpu.roll(jnp.where(two, grad, 0.0), count - 2, 0)
        held[:, :channels] = low(back_product * x_part)
        held[:, channels : 2 * channels] = low(back * conv_sum)
        held[:, 2 * channels :] = low(back_product * b_part)

    back_projected = held[...]
    plane = NY * rows
    grad_in = low(dot_columns(normed_ref[...], back_projected))
    grad_out = low(dot_columns(branch_part_ref[...], gated_ref[...]))
    for z in range(NZ):
        part = slice(z * plane, (z + 1) * plane)
        grads_ref[:, z, :, : 3 * channels] = grad_in[part].reshape(NY, rows, 3 * channels)
        grads_ref[:, z, :, 3 * channels :] = grad_out[part].reshape(NY, rows, channels)
    back_normed = dot_rows(back_projected, weights_part_ref[:, : 3 * channels])
    back_ref[...] = back_normed
    unit = tokens_ref[...].astype(jnp.float32) * scale_ref[...]
    gain_ref[...] = jnp.sum(back_normed * unit, axis=0, keepdims=True)


def mixer_pass(branch, weights, projected, masks, taps, gated, scale, normed, tokens):
    count, width = branch.shape
    channels = gated.shape[1]
    rows = width // N_DP
    block = width // NX
    whole = lambda i: (0, 0)
    column = pl.BlockSpec((count, block), lambda i: (0, i))
    return pl.pallas_call(
        mixer_kernel,
        grid=(NX,),
        in_specs=[
            pl.BlockSpec(branch.shape, whole),
            pl.BlockSpec(weights.shape, whole),
            pl.BlockSpec(projected.shape, whole),
            pl.BlockSpec(masks.shape, whole),
            pl.BlockSpec(taps.shape, whole),
            pl.BlockSpec(gated.shape, whole),
            pl.BlockSpec(scale.shape, whole),
            column,
            pl.BlockSpec((block, weights.shape[1]), lambda i: (i, 0)),
            column,
            column,
        ],
        out_specs=[
            pl.BlockSpec((NY, NZ, rows, 4 * channels), lambda i: (i, 0, 0, 0)),
            column,
            pl.BlockSpec((1, block), lambda i: (0, i)),
            pl.BlockSpec(taps.shape, whole),
        ],
        out_shape=[
            jax.ShapeDtypeStruct((NX * NY, NZ, rows, 4 * channels), jnp.bfloat16),
            jax.ShapeDtypeStruct((count, width), jnp.float32),
            jax.ShapeDtypeStruct((1, width), jnp.float32),
            jax.ShapeDtypeStruct(taps.shape, jnp.float32),
        ],
        scratch_shapes=[pltpu.VMEM((count, 3 * channels), jnp.bfloat16)],
        compiler_params=pltpu.CompilerParams(vmem_limit_bytes=VMEM_BYTES),
        cost_estimate=pl.CostEstimate(
            flops=16 * count * width * channels,
            bytes_accessed=20 * count * width,
            transcendentals=0,
        ),
        name="mixer_pass",
    )(branch, weights, projected, masks, taps, gated, scale, branch, weights, normed, tokens)


def pieces(value):
    high = lax.reduce_precision(value, 8, 7)
    rest = value - high
    middle = lax.reduce_precision(rest, 8, 7)
    return [low(high), low(middle), low(rest - middle)]


def shards(
    tokens_in,
    cotangent,
    segment_ids,
    in_weight,
    out_weight,
    gate_up_weight,
    down_weight,
    conv_weight,
    norm_gains,
    in_first,
    in_second,
    out_first,
    out_second,
    gate_up_first,
    gate_up_second,
    down_first,
    down_second,
    conv_first,
    conv_second,
    gains_first,
    gains_second,
):
    rows, length, width = tokens_in.shape
    count = rows * length
    taps_n, channels = conv_weight.shape
    units = gate_up_weight.shape[2]
    own_rows = gate_up_weight.shape[1]
    part_units = units // NZ
    core = lax.axis_index("tensor") % 2
    near = (lax.axis_index("dp") // NY) % NZ

    mix_cols = 4 * channels
    low_mix = jnp.concatenate(
        [
            in_weight[0],
            in_weight[1],
            in_weight[2],
            out_weight.T,
            jnp.pad(norm_gains.T, ((0, 0), (0, 126))),
        ],
        axis=1,
    )
    low_mix = low(low_mix)
    low_mix = jnp.stack(in_order(low_mix, swap_near(low_mix), near), axis=0)
    low_mix, gate_up_early, down_early, cotangent, tokens_in, segment_ids = (
        lax.optimization_barrier(
            (low_mix, gate_up_weight, down_weight, cotangent, tokens_in, segment_ids)
        )
    )
    low_ffn = low(jnp.concatenate([gate_up_early, down_early.T[None]], axis=0))
    keep = packed(lax.dynamic_slice_in_dim(low_ffn, near * part_units, part_units, 2))
    give = packed(lax.dynamic_slice_in_dim(low_ffn, (1 - near) * part_units, part_units, 2))
    take = swap_near(give)
    low_ffn = jnp.stack(in_order(keep, take, near), axis=0)
    ffn_copies = spread_pass(low_ffn)
    back_out = cotangent.reshape(count, width)
    back_own, back_other = halves(back_out, core)
    back_near = swap_near(back_own)
    back_twin = swap_core(back_near)

    flat = wide(tokens_in.reshape(count, width))
    flat_half = halves(flat, core)[0]
    seg_flat = segment_ids.reshape(count)
    place = lax.iota(jnp.int32, count) % length
    mask_one = ((place >= 1) & (seg_flat == jnp.roll(seg_flat, 1)))[:, None]
    mask_two = ((place >= 2) & (seg_flat == jnp.roll(seg_flat, 2)))[:, None]
    masks = wide(jnp.concatenate([mask_one, mask_two], axis=1))
    scale_one = lax.rsqrt(jnp.mean(flat * flat, axis=-1, keepdims=True) + epsilon_norm)

    mix_full = exchange(jnp.broadcast_to(low_mix[None], (NX * NY,) + low_mix.shape))
    mix_full, ffn_copies, back_near, back_twin = lax.optimization_barrier(
        (mix_full, ffn_copies, back_near, back_twin)
    )
    ffn_full = exchange(ffn_copies)
    mix_full = mix_full.reshape(NX, NY, NZ, own_rows, -1).transpose(0, 2, 1, 3, 4).reshape(width, -1)
    in_full = mix_full[:, : 3 * channels]
    out_full = mix_full[:, 3 * channels : mix_cols]
    gains_value = wide(mix_full[:, mix_cols : mix_cols + 2]).T


    def mixer_local(projected, taps):
        product = projected[:, :channels] * projected[:, 2 * channels :]
        conv_sum = taps[0] * product + taps[1] * jnp.where(
            mask_one, jnp.roll(product, 1, axis=0), 0.0
        )
        conv_sum = conv_sum + taps[2] * jnp.where(mask_two, jnp.roll(product, 2, axis=0), 0.0)
        return projected[:, channels : 2 * channels] * conv_sum

    normed_one = low(rms_gain(flat, gains_value[0]))
    projected = product_of("td,dc->tc", normed_one, in_full)
    gated = low(mixer_local(projected, conv_weight))
    middle = flat_half + sum_four(product_of("tc,dc->td", gated, out_full), core)
    normed_two_f, norm_two_pull = jax.vjp(rms_gain, middle, gains_value[1])
    normed_two = low(normed_two_f)
    normed_near = swap_near(normed_two)
    back_four = jnp.concatenate([back_own, back_near, back_other, back_twin], axis=0)
    normed_near, ffn_full, back_four, masks, scale_one = lax.optimization_barrier(
        (normed_near, ffn_full, back_four, masks, scale_one)
    )
    normed_two = jnp.concatenate(
        [normed_two, normed_near, swap_core(normed_two), swap_core(normed_near)], axis=0
    )

    back_gate, back_up, hidden, back_keep, back_give = hidden_pass(
        normed_two, back_four, ffn_full
    )
    back_pair = back_keep + wide(swap_core(back_give))
    back_pair, back_gate, back_up, hidden = lax.optimization_barrier(
        (back_pair, back_gate, back_up, hidden)
    )
    grad_ffn, ffn_keep, ffn_give = grads_pass(
        normed_two, back_four, back_gate, back_up, hidden, ffn_full
    )
    back_normed_two = back_pair[: count // 2] + wide(swap_near(low(back_pair[count // 2 :])))
    back_normed_two, grad_ffn = lax.optimization_barrier((back_normed_two, grad_ffn))
    back_normed_two = across_high(back_normed_two)
    grad_ffn = exchange(grad_ffn)

    ffn_keep, ffn_give, back_normed_two = lax.optimization_barrier(
        (ffn_keep, ffn_give, back_normed_two)
    )
    ffn_pair = ffn_keep + swap_core(ffn_give)
    ffn_half = ffn_pair[: count // 2] + wide(swap_near(low(ffn_pair[count // 2 :])))

    back_middle_norm, grad_gain_two = norm_two_pull(back_normed_two)
    back_middle = wide(back_own) + back_middle_norm
    back_branch = low(back_middle)
    back_branch = joined(back_branch, swap_core(back_branch), core)
    grad_mix, back_normed_one, grad_gain_one, grad_conv = mixer_pass(
        back_branch,
        mix_full,
        projected,
        masks,
        conv_weight,
        gated,
        scale_one,
        normed_one,
        tokens_in.reshape(count, width),
    )
    grad_gains = jnp.concatenate([grad_gain_one, 0.5 * grad_gain_two[None]], axis=0)
    grad_gains = grad_gains.reshape(2, N_DP, own_rows).transpose(1, 0, 2).reshape(N_DP, -1)
    grad_conv = jnp.broadcast_to(grad_conv.reshape(1, -1), (N_DP, grad_conv.size))
    small_size = grad_gains.shape[1] + grad_conv.shape[1]
    small = jnp.concatenate([grad_gains, grad_conv], axis=1)
    small = jnp.pad(small, ((0, 0), (0, 1024 - small_size))).reshape(N_DP, 8, 128)
    small = jnp.concatenate(
        pieces(small) + [jnp.zeros((N_DP, own_rows - 24, 128), jnp.bfloat16)], axis=1
    )
    grad_mix = jnp.concatenate([grad_mix, to_planes(small.reshape(width, 128))], axis=3)
    own, other = halves(back_normed_one, core)
    back_normed_one = own + swap_core(other)
    grad_ffn, grad_mix, back_normed_one = lax.optimization_barrier(
        (grad_ffn, grad_mix, back_normed_one)
    )
    red_mix = jnp.sum(wide(exchange(grad_mix)), axis=0)
    keep = lax.dynamic_index_in_dim(red_mix, near, 0, keepdims=False)
    red_mix = keep + swap_near(lax.dynamic_index_in_dim(red_mix, 1 - near, 0, keepdims=False))
    back_normed_one = across_high(back_normed_one)
    grad_ffn, back_normed_one, ffn_half = lax.optimization_barrier(
        (grad_ffn, back_normed_one, ffn_half)
    )
    red_ffn = whole_units(jnp.sum(wide(grad_ffn), axis=0), near)
    result = middle + across_high(ffn_half)
    result = joined(result, swap_core(result), core)
    back_tokens_norm = jax.vjp(rms_gain, flat_half, gains_value[0])[1](back_normed_one)[0]
    back_tokens = back_middle + back_tokens_norm
    back_tokens = joined(back_tokens, swap_core(back_tokens), core)

    red_small = jnp.sum(red_mix[:24, mix_cols:].reshape(3, 1024), axis=0)
    red_gains = red_small[: norm_gains.size].reshape(norm_gains.shape)
    red_gains = jnp.sum(lax.all_gather(red_gains, "tensor"), axis=0)
    conv_total = red_small[norm_gains.size : small_size].reshape(conv_weight.shape)
    red_in = red_mix[:, : 3 * channels].reshape(-1, 3, channels).transpose(1, 0, 2)
    red_out = red_mix[:, 3 * channels : mix_cols].T
    red_gate_up = red_ffn[:2]
    red_down = red_ffn[2].T
    rate_wide = 0.8 / D**0.5
    rate_down = 0.8 / FF**0.5
    in_new = adam_step(in_weight, red_in, in_first, in_second, rate_wide, 0.1)
    out_new = adam_step(out_weight, red_out, out_first, out_second, rate_wide, 0.1)
    gate_up_new = adam_step(
        gate_up_weight, red_gate_up, gate_up_first, gate_up_second, rate_wide, 0.1
    )
    down_new = adam_step(down_weight, red_down, down_first, down_second, rate_down, 0.1)
    conv_new = adam_step(conv_weight, conv_total, conv_first, conv_second, 1.0, 0.0)
    gains_new = adam_step(norm_gains, red_gains, gains_first, gains_second, 0.3, 0.0)
    return (
        result.reshape(rows, length, width),
        back_tokens.reshape(rows, length, width),
        in_new[0],
        in_new[1],
        in_new[2],
        out_new[0],
        out_new[1],
        out_new[2],
        gate_up_new[0],
        gate_up_new[1],
        gate_up_new[2],
        down_new[0],
        down_new[1],
        down_new[2],
        conv_new[0],
        conv_new[1],
        conv_new[2],
        gains_new[0],
        gains_new[1],
        gains_new[2],
    )


def solution(mesh):
    in_specs = (
        P("dp", None, None),
        P("dp", None, None),
        P("dp", None),
        P(None, "dp", "tensor"),
        P("tensor", "dp"),
        P(None, "dp", "tensor"),
        P("tensor", "dp"),
        P(None, "tensor"),
        P(None, "dp"),
        P(None, "dp", "tensor"),
        P(None, "dp", "tensor"),
        P("tensor", "dp"),
        P("tensor", "dp"),
        P(None, "dp", "tensor"),
        P(None, "dp", "tensor"),
        P("tensor", "dp"),
        P("tensor", "dp"),
        P(None, "tensor"),
        P(None, "tensor"),
        P(None, "dp"),
        P(None, "dp"),
    )
    out_specs = (
        P("dp", None, None),
        P("dp", None, None),
        P(None, "dp", "tensor"),
        P(None, "dp", "tensor"),
        P(None, "dp", "tensor"),
        P("tensor", "dp"),
        P("tensor", "dp"),
        P("tensor", "dp"),
        P(None, "dp", "tensor"),
        P(None, "dp", "tensor"),
        P(None, "dp", "tensor"),
        P("tensor", "dp"),
        P("tensor", "dp"),
        P("tensor", "dp"),
        P(None, "tensor"),
        P(None, "tensor"),
        P(None, "tensor"),
        P(None, "dp"),
        P(None, "dp"),
        P(None, "dp"),
    )
    return jax.shard_map(shards, mesh=mesh, in_specs=in_specs, out_specs=out_specs, check_vma=False)
```
